128 devices in a mesh: row: 4 (over x), col: 32 (over y, z, core).
Axes of the slice: x: 4, y: 4, z: 4, core: 2. Of those that a mesh axis runs over, the one named last changes fastest.
Arguments:
- features: bfloat16 [262144, 128], P(('row', 'col')), may hold values from -6 to 6
- self_one: bfloat16 [128, 256], replicated, may hold values from -0.5 to 0.5
- neigh_one: bfloat16 [128, 256], replicated, may hold values from -0.5 to 0.5
- self_two: bfloat16 [256, 172], replicated, may hold values from -0.375 to 0.375
- neigh_two: bfloat16 [256, 172], replicated, may hold values from -0.375 to 0.375
- tile_values: bfloat16 [24576, 128, 128], P(('row', 'col')), may hold values from 0 to 0.059814453
- tile_rows: int32 [128, 192], P(('row', 'col')), may hold values from 0 to 15, as said below
- tile_cols: int32 [128, 192], P(('row', 'col')), may hold values from 0 to 31
- tile_count: int32 [128], P(('row', 'col')), may hold values from 1 to 192, as said below
- part_size: int32 [128], P(('row', 'col')), may hold values from 256 to 2048, as said below
- send_rows: int32 [128, 128, 16], P(('row', 'col')), may hold values from 0 to 2047, as said below
- send_count: int32 [128, 128], replicated, may hold values from 0 to 16, as said below
- labels: int32 [262144], P(('row', 'col')), may hold values from 0 to 171
- train_mask: int32 [262144], P(('row', 'col')), may hold values 0 or 1
- stale_hidden: bfloat16 [262144, 256], P(('row', 'col')), may hold values from -6 to 6
- stale_grads: bfloat16 [262144, 256], P(('row', 'col')), may hold values from -0.059814453 to 0.059814453
Outputs:
- grad_self_one: float32 [128, 256], replicated
- grad_neigh_one: float32 [128, 256], replicated
- grad_self_two: float32 [256, 172], replicated
- grad_neigh_two: float32 [256, 172], replicated
- fresh_hidden: bfloat16 [262144, 256], P(('row', 'col'))
- fresh_grads: bfloat16 [262144, 256], P(('row', 'col'))
The draws below stay inside these ranges and needn't reach their ends.
Inputs may be any that keep to these rules, and one draw needn't show every extreme that they name: `part_size`: one part holds exactly 2048 live nodes. `tile_count`: the largest part uses all 192 tile slots. `tile_rows`: tiles lie in row blocks that hold live nodes. `send_rows`: every entry is below the sending part's size. `send_count`: A part sends nothing to itself; some part receives 16 rows from every other part.
All inputs are finite; a program needn't handle non-finite values. No bound on the sum of `train_mask` on one device may be relied on, other than what follows from the above.
Results may differ from the reference program's by a relative error of at most 0.0095.
Values may be sent and summed in bfloat16 or wider, within the bound.
A program may use at most 128 MiB of HBM per device.

```python
import jax
import jax.numpy as jnp
from jax import lax

F_IN = 128
HID = 256
CLASSES = 172
BLOCK = 128
NODE_CAP = 2048
SLOT = 16
TILES = 192
HALO = 2048
NODES = 262144
HALO_ALL = 262144
ALL_TILES = 24576
N_ROW = 4
N_COL = 32


def part_sizes(key):
    parts = N_ROW * N_COL
    first, second = jax.random.split(key)
    small = jax.random.randint(first, (parts,), NODE_CAP // 8, NODE_CAP // 2 + 1)
    largest = jax.random.randint(second, (), 0, parts)
    return jnp.where(jnp.arange(parts) == largest, NODE_CAP, small).astype(jnp.int32)


def draw_part_size(key, part):
    return part_sizes(key)


def draw_tile_count(key, part):
    sizes = part_sizes(key)
    key = jax.random.fold_in(key, 11)
    jitter = jax.random.randint(key, sizes.shape, 0, max(1, TILES // 16))
    counts = jnp.clip(TILES * sizes // NODE_CAP - jitter, 1, TILES)
    return jnp.where(sizes == NODE_CAP, TILES, counts).astype(jnp.int32)


def draw_tile_rows(key, part):
    sizes = part_sizes(key)
    key = jax.random.fold_in(key, 13)
    live_blocks = (sizes + BLOCK - 1) // BLOCK
    return jax.random.randint(key, (N_ROW * N_COL, TILES), 0, live_blocks[:, None]).astype(jnp.int32)


def draw_send_rows(key, part):
    sizes = part_sizes(key)
    key = jax.random.fold_in(key, 17)
    parts = N_ROW * N_COL
    return jax.random.randint(key, (parts, parts, SLOT), 0, sizes[:, None, None]).astype(jnp.int32)


def draw_send_count(key, part):
    key = jax.random.fold_in(key, 19)
    parts = N_ROW * N_COL
    first, second = jax.random.split(key)
    counts = jax.random.randint(first, (parts, parts), 0, SLOT + 1)
    full = jax.random.randint(second, (), 0, parts)
    index = jnp.arange(parts)
    counts = jnp.where(index[None, :] == full, SLOT, counts)
    counts = jnp.where(index[:, None] == index[None, :], 0, counts)
    return counts.astype(jnp.int32)


def touch_ends(drawn, own_key, least, high):
    index_at = [jax.random.randint(jax.random.fold_in(own_key, axis), (), 0, length) for axis, length in enumerate(drawn.shape)]
    main_axis = drawn.shape.index(max(drawn.shape))
    neighbour = index_at[:main_axis] + [(index_at[main_axis] + 1) % drawn.shape[main_axis]] + index_at[main_axis + 1:]
    return drawn.at[tuple(index_at)].set(least).at[tuple(neighbour)].set(high)


def level_of(own_key, shape, cuts, least, high):
    def one(position, shards_of):
        draws = jax.random.uniform(jax.random.fold_in(jax.random.fold_in(own_key, 6), position), (shards_of,), jnp.float32, least / len(cuts), high / len(cuts))
        return jnp.repeat(jnp.exp(draws), shape[position] // shards_of).reshape((-1,) + (1,) * (len(shape) - position - 1))

    level = one(*cuts[0])
    for cut in cuts[1:]:
        level = level * one(*cut)
    return level


def noise(rng, shape, scale, limit, cuts=(), dtype=jnp.bfloat16):
    gain = level_of(rng, shape, cuts, -0.22, 0.18) if cuts else 1.0
    result = jax.random.normal(rng, shape, jnp.float32) * scale * gain
    return jnp.minimum(jnp.maximum(result, -limit), limit).astype(dtype)


def setup_inputs(seed: int = 0) -> dict:
    keys = jax.random.split(jax.random.key(seed), 17)
    features = noise(keys[0], (NODES, F_IN), 1.0, 6.0, ((0, 128),))
    self_one = noise(keys[1], (F_IN, HID), F_IN ** -0.5, 0.5)
    neigh_one = noise(keys[2], (F_IN, HID), F_IN ** -0.5, 0.5)
    self_two = noise(keys[3], (HID, CLASSES), HID ** -0.5, 0.375)
    neigh_two = noise(keys[4], (HID, CLASSES), HID ** -0.5, 0.375)
    tile_values = jnp.clip(0.059814453 * jax.random.uniform(keys[5], (ALL_TILES, BLOCK, BLOCK), jnp.float32) ** level_of(keys[5], (ALL_TILES, BLOCK, BLOCK), ((0, 128),), -0.2, 0.2), 0.0, 0.059814453).astype(jnp.bfloat16)
    tile_rows = draw_tile_rows(jax.random.fold_in(keys[16], 71), 0)
    tile_cols = touch_ends(jax.random.randint(keys[7], (N_ROW * N_COL, TILES), 0, (NODE_CAP + HALO) // BLOCK), jax.random.fold_in(keys[7], 1), 0, ((NODE_CAP + HALO) // BLOCK) - 1).astype(jnp.int32)
    tile_count = draw_tile_count(jax.random.fold_in(keys[16], 71), 0)
    part_size = draw_part_size(jax.random.fold_in(keys[16], 71), 0)
    send_rows = draw_send_rows(jax.random.fold_in(keys[16], 71), 0)
    send_count = draw_send_count(jax.random.fold_in(keys[16], 71), 0)
    labels = touch_ends(jax.random.randint(keys[12], (NODES,), 0, CLASSES), jax.random.fold_in(keys[12], 1), 0, CLASSES - 1).astype(jnp.int32)
    train_mask = touch_ends((jax.random.randint(keys[13], (NODES,), 0, 2) < 1).astype(jnp.int32), jax.random.fold_in(keys[13], 1), 0, 1)
    stale_hidden = noise(keys[14], (HALO_ALL, HID), 1.0, 6.0, ((0, 128),))
    stale_grads = noise(keys[15], (HALO_ALL, HID), 0.01, 0.059814453, ((0, 128),))
    return {"features": features, "self_one": self_one, "neigh_one": neigh_one, "self_two": self_two, "neigh_two": neigh_two, "tile_values": tile_values, "tile_rows": tile_rows, "tile_cols": tile_cols, "tile_count": tile_count, "part_size": part_size, "send_rows": send_rows, "send_count": send_count, "labels": labels, "train_mask": train_mask, "stale_hidden": stale_hidden, "stale_grads": stale_grads}


loss_scale = 1.0 / 32.0


def aggregate(whole, values, rows, cols, count, nblocks):
    width = whole.shape[1]
    block = values.shape[1]
    pieces = whole.reshape(-1, block, width)[cols]
    product = jnp.einsum('tij,tjf->tif', values.astype(jnp.float32), pieces.astype(jnp.float32))
    live = jnp.arange(values.shape[0]) < count
    onehot = ((rows[:, None] == jnp.arange(nblocks)[None, :]) & live[:, None]).astype(jnp.float32)
    summed = jnp.einsum('tr,tif->rif', onehot, product, precision=lax.Precision.HIGHEST)
    return summed.reshape(nblocks * block, width)


def aggregate_back(grad, values, rows, cols, count, nblocks):
    width = grad.shape[1]
    block = values.shape[1]
    pieces = grad.reshape(-1, block, width)[rows]
    product = jnp.einsum('tji,tjf->tif', values.astype(jnp.float32), pieces.astype(jnp.float32))
    live = jnp.arange(values.shape[0]) < count
    onehot = ((cols[:, None] == jnp.arange(nblocks)[None, :]) & live[:, None]).astype(jnp.float32)
    summed = jnp.einsum('tc,tif->cif', onehot, product, precision=lax.Precision.HIGHEST)
    return summed.reshape(nblocks * block, width)


def boundary(values3, send_rows, send_count):
    parts = values3.shape[0]
    slot = send_rows.shape[2]
    source = jnp.arange(parts).astype(jnp.int32)[:, None, None]
    picked = values3[source, send_rows]
    live = jnp.arange(slot)[None, None, :] < send_count[:, :, None]
    picked = jnp.where(live[..., None], picked, 0)
    return jnp.transpose(picked, (1, 0, 2, 3)).reshape(parts, parts * slot, values3.shape[2])


def reference(features, self_one, neigh_one, self_two, neigh_two, tile_values, tile_rows, tile_cols, tile_count, part_size, send_rows, send_count, labels, train_mask, stale_hidden, stale_grads):
    parts = N_ROW * N_COL
    row_blocks = NODE_CAP // BLOCK
    all_blocks = (NODE_CAP + HALO) // BLOCK
    feats3 = features.reshape(parts, NODE_CAP, F_IN)
    node_index = jnp.arange(NODE_CAP)[None, :]
    live_rows = node_index < part_size[:, None]
    feats3 = jnp.where(live_rows[..., None], feats3, 0)
    halo_feats = boundary(feats3, send_rows, send_count)
    tiles4 = tile_values.reshape(parts, TILES, BLOCK, BLOCK)
    stale_h3 = stale_hidden.reshape(parts, HALO, HID)
    stale_g3 = stale_grads.reshape(parts, HALO, HID)
    labels2 = labels.reshape(parts, NODE_CAP)
    mask2 = train_mask.reshape(parts, NODE_CAP)

    def one_part(items):
        index, own, halo_in, tiles, rows, cols, count, size, my_rows, stale_h, stale_g, my_labels, my_mask = items
        out_count = send_count[index]
        in_count = send_count[:, index]
        recv_live = (jnp.arange(SLOT)[None, :] < in_count[:, None]).reshape(HALO)
        send_live = (jnp.arange(SLOT)[None, :] < out_count[:, None]).reshape(HALO)
        row_live = jnp.arange(NODE_CAP) < size
        whole = jnp.concatenate([own, halo_in], axis=0)
        agg_one = aggregate(whole, tiles, rows, cols, count, row_blocks).astype(jnp.bfloat16)
        pre_one = jnp.dot(own, self_one, preferred_element_type=jnp.float32) + jnp.dot(agg_one, neigh_one, preferred_element_type=jnp.float32)
        hidden = jnp.where(row_live[:, None], jax.nn.silu(pre_one), 0.0).astype(jnp.bfloat16)
        stale_live = jnp.where(recv_live[:, None], stale_h, 0)
        whole_two = jnp.concatenate([hidden, stale_live], axis=0)
        agg_two = aggregate(whole_two, tiles, rows, cols, count, row_blocks).astype(jnp.bfloat16)
        logits = jnp.dot(hidden, self_two, preferred_element_type=jnp.float32) + jnp.dot(agg_two, neigh_two, preferred_element_type=jnp.float32)
        expo = jnp.exp(logits - jnp.max(logits, axis=1, keepdims=True))
        probability = expo / jnp.sum(expo, axis=1, keepdims=True)
        weight = jnp.where(row_live & (my_mask > 0), loss_scale, 0.0).astype(jnp.float32)
        target = (my_labels[:, None] == jnp.arange(CLASSES)[None, :]).astype(jnp.float32)
        grad_logits = ((probability - target) * weight[:, None]).astype(jnp.bfloat16)
        grad_self2 = jnp.dot(hidden.T, grad_logits, preferred_element_type=jnp.float32)
        grad_neigh2 = jnp.dot(agg_two.T, grad_logits, preferred_element_type=jnp.float32)
        back_self = jnp.dot(grad_logits, self_two.T, preferred_element_type=jnp.float32)
        grad_agg = jnp.dot(grad_logits, neigh_two.T, preferred_element_type=jnp.float32).astype(jnp.bfloat16)
        spread = aggregate_back(grad_agg, tiles, rows, cols, count, all_blocks)
        returned = jnp.where(recv_live[:, None], spread[NODE_CAP:], 0.0).astype(jnp.bfloat16)
        incoming = jnp.where(send_live[:, None], stale_g.astype(jnp.float32), 0.0)
        scattered = jnp.zeros((NODE_CAP, HID), jnp.float32).at[my_rows.reshape(HALO)].add(incoming)
        grad_hidden = back_self + spread[:NODE_CAP] + scattered
        sigma = jax.nn.sigmoid(pre_one)
        slope = sigma * (1.0 + pre_one * (1.0 - sigma))
        grad_pre = jnp.where(row_live[:, None], grad_hidden * slope, 0.0).astype(jnp.bfloat16)
        grad_self1 = jnp.dot(own.T, grad_pre, preferred_element_type=jnp.float32)
        grad_neigh1 = jnp.dot(agg_one.T, grad_pre, preferred_element_type=jnp.float32)
        return hidden, returned, grad_self1, grad_neigh1, grad_self2, grad_neigh2

    hidden_all, returned_all, gs1, gn1, gs2, gn2 = lax.map(one_part, (jnp.arange(parts).astype(jnp.int32), feats3, halo_feats, tiles4, tile_rows, tile_cols, tile_count, part_size, send_rows, stale_h3, stale_g3, labels2, mask2))
    fresh_hidden = boundary(hidden_all, send_rows, send_count).reshape(parts * HALO, HID)
    fresh_grads = jnp.transpose(returned_all.reshape(parts, parts, SLOT, HID), (1, 0, 2, 3)).reshape(parts * HALO, HID)
    return (jnp.sum(gs1, axis=0), jnp.sum(gn1, axis=0), jnp.sum(gs2, axis=0), jnp.sum(gn2, axis=0), fresh_hidden, fresh_grads)
```

```python
import functools

import jax
import jax.numpy as jnp
from jax import lax
from jax.experimental import pallas as pl
from jax.experimental.pallas import tpu as pltpu
from jax.sharding import PartitionSpec as P

MESH = pl.DeviceIdType.MESH
F32 = jnp.float32
BF16 = jnp.bfloat16
NODE = 2048
HALO = 2048
BLK = 128
SLOT = 16
PARTS = 128
ROWS = 4
COLS = 32
TILES = 192
F_IN = 128
HID = 256
CLS = 172
CLSP = 176
CH = 512
NCH = 4
PIECES = 76
LOSS_SCALE = 1.0 / 32.0


def dot(a, b):
    return lax.dot_general(a, b, (((1,), (0,)), ((), ())), preferred_element_type=F32)


def dot_nt(a, b):
    return lax.dot_general(a, b, (((1,), (1,)), ((), ())), preferred_element_type=F32)


def at(start, size, mult=None):
    return pl.ds(pl.multiple_of(start, mult or size), size)


def device(index):
    return (index // COLS, lax.rem(index, COLS))


def owner_of(piece):
    return jnp.where(piece < 64, 2 * piece, 10 * (piece - 64) + 1)


def kernel(
    nxt, first, size_ref,
    feat_hbm, tiles_hbm, stale_hbm, grads_hbm,
    w1s_ref, w1n_ref, w2s_ref, w2n_ref, rows_ref, count_ref, labels_ref, mask_ref,
    gs1_ref, gn1_ref, gs2_ref, gn2_ref, fh_hbm, fg_hbm,
    adj, pick, chain, tbuf, own, both, halo, hidden, stale, grad_t, acc1, acc2, agg2,
    gl_t, ga_t, gp_t, recv_mask, send1, send2, send3, w2, contrib, part_in, result, small,
    tile_sem, load_sem, ssem, rsem, local_sem,
):
    my_row = lax.axis_index("row")
    my_col = lax.axis_index("col")
    me = my_row * COLS + my_col
    size = size_ref[0]

    barrier = pltpu.get_barrier_semaphore()

    def greet(i, c):
        pl.semaphore_signal(
            barrier, inc=1, device_id=device(jnp.bitwise_xor(me, i)), device_id_type=MESH
        )
        return c

    lax.fori_loop(1, PARTS, greet, 0)

    def load_tiles(k):
        return pltpu.make_async_copy(
            tiles_hbm.at[pl.ds(k * 48, 48)], tbuf.at[k % 2], tile_sem.at[k % 2]
        )

    load_own = pltpu.make_async_copy(feat_hbm, own, load_sem.at[0])
    load_own.start()
    load_tiles(3).start()
    load_tiles(2).start()
    load_stale = pltpu.make_async_copy(stale_hbm, stale, load_sem.at[1])
    load_stale.start()
    load_grads = pltpu.make_async_copy(grads_hbm, hidden, load_sem.at[2])
    load_grads.start()

    w2[...] = jnp.zeros_like(w2)
    w2[0:HID, 0:CLS] = w2s_ref[...]
    w2[HID : 2 * HID, 0:CLS] = w2n_ref[...]

    lanes128 = lax.broadcasted_iota(jnp.int32, (PARTS, BLK), 0)
    is_me = jnp.where(lanes128 == me, 1.0, 0.0).astype(BF16)
    counts = count_ref[...].astype(F32)
    in_count = dot(counts.astype(BF16), is_me).astype(BF16)
    out_count = dot(jnp.transpose(counts).astype(BF16), is_me).astype(BF16)
    rows = rows_ref[...]
    high = (rows // 128).astype(F32).astype(BF16)
    low = (rows % 128).astype(F32).astype(BF16)
    spread_ones = jnp.ones((SLOT, BLK), BF16)

    def build_pick(k, c):
        h = lax.broadcasted_iota(jnp.int32, (CH, PARTS), 0) + k * CH
        q = lax.broadcasted_iota(jnp.int32, (CH, PARTS), 1)
        expand = jnp.where(h // SLOT == q, 1.0, 0.0).astype(BF16)
        hs = lax.broadcasted_iota(jnp.int32, (CH, SLOT), 0)
        js = lax.broadcasted_iota(jnp.int32, (CH, SLOT), 1)
        slot_is = hs % SLOT == js
        high_b = dot(jnp.where(slot_is, dot(expand, high), 0.0).astype(BF16), spread_ones)
        low_b = dot(jnp.where(slot_is, dot(expand, low), 0.0).astype(BF16), spread_ones)
        j_of = (h % SLOT).astype(F32)
        live = j_of < dot(expand, out_count)
        recv_mask[at(k * CH, CH), :] = jnp.where(j_of < dot(expand, in_count), 1.0, 0.0)
        key = jnp.where(live & (low_b == q.astype(F32)), high_b, -1.0)
        for b in range(NODE // BLK):
            pick[at(k * CH, CH), b * BLK : (b + 1) * BLK] = jnp.where(
                key == float(b), 1.0, 0.0
            ).astype(BF16)
        return c

    lax.fori_loop(0, NCH, build_pick, 0)

    load_own.wait()

    def mask_own(k, c):
        row = lax.broadcasted_iota(jnp.int32, (CH, F_IN), 0) + k * CH
        kept = jnp.where(row < size, own[at(k * CH, CH), :].astype(F32), 0.0).astype(BF16)
        own[at(k * CH, CH), :] = kept
        both[at(k * CH, CH), 0:F_IN] = kept
        return c

    lax.fori_loop(0, NCH, mask_own, 0)

    def gather_feats(k, c):
        send1[at(k * CH, CH), :] = dot(pick[at(k * CH, CH), :], own[...]).astype(BF16)
        return c

    lax.fori_loop(0, NCH, gather_feats, 0)

    pl.semaphore_wait(barrier, PARTS - 1)

    def piece_of(index):
        return at(index * SLOT, SLOT)

    def send_to(src, dst, which, d):
        pltpu.make_async_remote_copy(
            src_ref=src.at[piece_of(d)],
            dst_ref=dst.at[piece_of(me)],
            send_sem=ssem.at[which],
            recv_sem=rsem.at[which],
            device_id=device(d),
            device_id_type=MESH,
        ).start()

    def send_feats(i, c):
        send_to(send1, halo, 0, jnp.bitwise_xor(me, i))
        return c

    lax.fori_loop(1, PARTS, send_feats, 0)
    halo[piece_of(me), :] = jnp.zeros((SLOT, F_IN), BF16)

    load_grads.wait()

    def turn_grads(k, c):
        grad_t[:, at(k * CH, CH)] = jnp.transpose(hidden[at(k * CH, CH), :])
        return c

    lax.fori_loop(0, NCH, turn_grads, 0)

    chain[TILES] = jnp.zeros((BLK, BLK), F32)
    for k in (3, 2, 1, 0):
        load_tiles(k).wait()

        def link(i, c, k=k):
            t = 47 - i
            chain[k * 48 + t] = tbuf[k % 2, t].astype(F32) + chain[nxt[k * 48 + t]]
            return c

        lax.fori_loop(0, 48, link, 0)
        if k >= 2:
            load_tiles(k - 2).start()

    def fill(r, c):
        for col in range(32):
            adj[at(r * BLK, BLK), col * BLK : (col + 1) * BLK] = chain[
                first[r * 32 + col]
            ].astype(BF16)
        return c

    lax.fori_loop(0, NODE // BLK, fill, 0)

    load_stale.wait()

    def mask_stale(k, c):
        live = recv_mask[at(k * CH, CH), :] > 0.0
        for half in range(2):
            cut = slice(half * BLK, (half + 1) * BLK)
            stale[at(k * CH, CH), cut] = jnp.where(
                live, stale[at(k * CH, CH), cut].astype(F32), 0.0
            ).astype(BF16)
        return c

    lax.fori_loop(0, NCH, mask_stale, 0)

    def early(k, c):
        cut = at(k * CH, CH)
        acc1[cut, :] = dot(adj[cut, 0:NODE], own[...])
        acc2[cut, :] = dot(adj[cut, NODE : NODE + HALO], stale[...])
        return c

    lax.fori_loop(0, NCH, early, 0)

    def wait_bytes(ref, sem):
        pltpu.make_async_copy(ref, ref, sem).wait()

    wait_bytes(halo.at[pl.ds(0, HALO - SLOT)], rsem.at[0])

    def first_layer(k, c):
        cut = at(k * CH, CH)
        agg = acc1[cut, :] + dot(adj[cut, NODE : NODE + HALO], halo[...])
        both[cut, F_IN : 2 * F_IN] = agg.astype(BF16)
        pre = dot(own[cut, :], w1s_ref[...]) + dot(agg.astype(BF16), w1n_ref[...])
        row = lax.broadcasted_iota(jnp.int32, (CH, HID), 0) + k * CH
        act = pre / (1.0 + jnp.exp(-pre))
        hidden[cut, :] = jnp.where(row < size, act, 0.0).astype(BF16)
        return c

    lax.fori_loop(0, NCH, first_layer, 0)

    def send_hidden(k, c):
        there = jnp.bitwise_xor(my_row, k)
        cut = at(there * CH, CH)
        send2[cut, :] = dot(pick[cut, :], hidden[...]).astype(BF16)

        def one(i, c2):
            d = there * COLS + jnp.bitwise_xor(my_col, i)

            @pl.when(d != me)
            def _():
                send_to(send2, fh_hbm, 1, d)

            return c2

        return lax.fori_loop(0, COLS, one, c)

    lax.fori_loop(0, NCH, send_hidden, 0)
    own_hidden = pltpu.make_async_copy(
        send2.at[piece_of(me)], fh_hbm.at[piece_of(me)], local_sem.at[0]
    )
    own_hidden.start()

    def second_agg(k, c):
        cut = at(k * CH, CH)
        agg2[cut, :] = (acc2[cut, :] + dot(adj[cut, 0:NODE], hidden[...])).astype(BF16)
        return c

    lax.fori_loop(0, NCH, second_agg, 0)

    gl_t[...] = jnp.zeros_like(gl_t)
    w2s_t = jnp.transpose(w2[0:HID, :])
    w2n_t = jnp.transpose(w2[HID : 2 * HID, :])

    def loss_grad(k, c):
        cut = at(k * CH, CH)
        logits = dot_nt(w2s_t, hidden[cut, :]) + dot_nt(w2n_t, agg2[cut, :])
        logits = logits[0:CLSP, :]
        cls = lax.broadcasted_iota(jnp.int32, (CLSP, CH), 0)
        logits = jnp.where(cls < CLS, logits, -jnp.inf)
        expo = jnp.exp(logits - jnp.max(logits, axis=0, keepdims=True))
        total = jnp.sum(expo, axis=0, keepdims=True)
        node = lax.broadcasted_iota(jnp.int32, (1, CH), 1) + k * CH
        weight = jnp.where((node < size) & (mask_ref[:, cut] > 0), LOSS_SCALE, 0.0)
        target = jnp.where(cls == labels_ref[:, cut], 1.0, 0.0)
        gl_t[0:CLSP, cut] = ((expo / total - target) * weight).astype(BF16)
        return c

    lax.fori_loop(0, NCH, loss_grad, 0)

    g2s = dot(gl_t[0:CLSP, :], hidden[...])
    g2n = dot(gl_t[0:CLSP, :], agg2[...])
    for b, (src, half) in enumerate(((g2s, 0), (g2s, 1), (g2n, 0), (g2n, 1))):
        contrib[512 + b * CLSP : 512 + (b + 1) * CLSP, :] = src[
            :, half * BLK : (half + 1) * BLK
        ].astype(BF16)

    def back_agg(k, c):
        cut = at(k * CH, CH)
        ga_t[:, cut] = dot(w2[HID : 2 * HID, :], gl_t[:, cut]).astype(BF16)
        return c

    lax.fori_loop(0, NCH, back_agg, 0)

    w1s_t = jnp.transpose(w1s_ref[...])
    w1n_t = jnp.transpose(w1n_ref[...])

    def back_first(k, c):
        cut = at(k * CH, CH)
        grad = dot(ga_t[...], adj[:, cut]) + dot(grad_t[...], pick[:, cut])
        grad = grad + dot(w2[0:HID, :], gl_t[:, cut])
        pre = dot_nt(w1s_t, both[cut, 0:F_IN]) + dot_nt(w1n_t, both[cut, F_IN : 2 * F_IN])
        sigma = 1.0 / (1.0 + jnp.exp(-pre))
        slope = sigma * (1.0 + pre * (1.0 - sigma))
        node = lax.broadcasted_iota(jnp.int32, (HID, CH), 1) + k * CH
        gp_t[:, cut] = jnp.where(node < size, grad * slope, 0.0).astype(BF16)
        return c

    lax.fori_loop(0, NCH, back_first, 0)

    g1 = dot(gp_t[...], both[...])
    contrib[0:HID, :] = g1[:, 0:F_IN].astype(BF16)
    contrib[HID : 2 * HID, :] = g1[:, F_IN : 2 * F_IN].astype(BF16)

    second = jnp.where(lax.rem(me, 2) == 0, -1, jnp.where(lax.rem(me - 1, 10) == 0, (me - 1) // 10, 12))
    my_piece = jnp.where(lax.rem(me, 2) == 0, me // 2, jnp.where(second < 12, 64 + second, PIECES))
    owns = my_piece < PIECES

    def send_piece(i, c):
        d = owner_of(i)

        @pl.when(d != me)
        def _():
            pltpu.make_async_remote_copy(
                src_ref=contrib.at[piece_of(i)],
                dst_ref=part_in.at[piece_of(me)],
                send_sem=ssem.at[3],
                recv_sem=rsem.at[3],
                device_id=device(d),
                device_id_type=MESH,
            ).start()

        return c

    lax.fori_loop(0, PIECES, send_piece, 0)

    @pl.when(owns)
    def _():
        part_in[piece_of(me), :] = contrib[piece_of(my_piece), :]

    def send_spread(k, c):
        there = jnp.bitwise_xor(my_row, k)
        cut = at(there * CH, CH)
        spread = dot(ga_t[...], adj[:, at(NODE + there * CH, CH)])
        spread = jnp.transpose(spread)
        live = recv_mask[cut, :] > 0.0
        for half in range(2):
            lanes = slice(half * BLK, (half + 1) * BLK)
            send3[cut, lanes] = jnp.where(live, spread[:, lanes], 0.0).astype(BF16)

        def one(i, c2):
            d = there * COLS + jnp.bitwise_xor(my_col, i)

            @pl.when(d != me)
            def _():
                send_to(send3, fg_hbm, 2, d)

            return c2

        return lax.fori_loop(0, COLS, one, c)

    send_spread(0, 0)

    @pl.when(owns)
    def _():
        wait_bytes(part_in.at[pl.ds(0, (PARTS - 1) * SLOT)], rsem.at[3])
        small[...] = jnp.zeros_like(small)

        def add(i, c):
            small[...] += part_in[piece_of(i), :].astype(F32)
            return c

        lax.fori_loop(0, PARTS, add, 0)
        result[piece_of(my_piece), :] = small[...].astype(BF16)

        def give(i, c):
            pltpu.make_async_remote_copy(
                src_ref=result.at[piece_of(my_piece)],
                dst_ref=result.at[piece_of(my_piece)],
                send_sem=ssem.at[4],
                recv_sem=rsem.at[4],
                device_id=device(jnp.bitwise_xor(me, i)),
                device_id_type=MESH,
            ).start()
            return c

        lax.fori_loop(1, PARTS, give, 0)

    lax.fori_loop(1, NCH, send_spread, 0)
    own_spread = pltpu.make_async_copy(
        send3.at[piece_of(me)], fg_hbm.at[piece_of(me)], local_sem.at[1]
    )
    own_spread.start()

    @pl.when(owns)
    def _():
        wait_bytes(part_in.at[pl.ds(0, (PARTS - 1) * SLOT)], ssem.at[4])
        wait_bytes(result.at[pl.ds(0, (PIECES - 1) * SLOT)], rsem.at[4])
        wait_bytes(contrib.at[pl.ds(0, (PIECES - 1) * SLOT)], ssem.at[3])

    @pl.when(jnp.logical_not(owns))
    def _():
        wait_bytes(result, rsem.at[4])
        wait_bytes(contrib, ssem.at[3])

    gs1_ref[...] = jnp.transpose(result[0:HID, :].astype(F32))
    gn1_ref[...] = jnp.transpose(result[HID : 2 * HID, :].astype(F32))
    for b, (dst, half) in enumerate(((gs2_ref, 0), (gs2_ref, 1), (gn2_ref, 0), (gn2_ref, 1))):
        block = result[512 + b * CLSP : 512 + (b + 1) * CLSP, :].astype(F32)
        block = jnp.concatenate([block, jnp.zeros((HID - CLSP, BLK), F32)], axis=0)
        dst[half * BLK : (half + 1) * BLK, :] = jnp.transpose(block)[:, 0:CLS]

    own_hidden.wait()
    own_spread.wait()
    wait_bytes(send1.at[pl.ds(0, HALO - SLOT)], ssem.at[0])
    for which, src, dst in ((1, send2, fh_hbm), (2, send3, fg_hbm)):
        wait_bytes(src.at[pl.ds(0, HALO - SLOT)], ssem.at[which])
        wait_bytes(dst.at[pl.ds(0, HALO - SLOT)], rsem.at[which])


def local(
    features, self_one, neigh_one, self_two, neigh_two, tile_values, tile_rows, tile_cols,
    tile_count, part_size, send_rows, send_count, labels, train_mask, stale_hidden, stale_grads,
):
    index = jnp.arange(TILES)
    live = index < tile_count[0]
    block = tile_rows[0] * 32 + tile_cols[0]
    later = (block[:, None] == block[None, :]) & (index[None, :] > index[:, None]) & live[None, :]
    nxt = jnp.min(jnp.where(later, index[None, :], TILES), axis=1).astype(jnp.int32)
    here = (jnp.arange(512)[:, None] == block[None, :]) & live[None, :]
    first = jnp.min(jnp.where(here, index[None, :], TILES), axis=1).astype(jnp.int32)

    smem = pl.BlockSpec(memory_space=pltpu.SMEM)
    vmem = pl.BlockSpec(memory_space=pltpu.VMEM)
    hbm = pl.BlockSpec(memory_space=pl.ANY)
    outs = pl.pallas_call(
        kernel,
        out_shape=(
            jax.ShapeDtypeStruct((F_IN, HID), F32),
            jax.ShapeDtypeStruct((F_IN, HID), F32),
            jax.ShapeDtypeStruct((HID, CLS), F32),
            jax.ShapeDtypeStruct((HID, CLS), F32),
            jax.ShapeDtypeStruct((HALO, HID), BF16),
            jax.ShapeDtypeStruct((HALO, HID), BF16),
        ),
        in_specs=[smem] * 3 + [hbm] * 4 + [vmem] * 8,
        out_specs=(vmem, vmem, vmem, vmem, hbm, hbm),
        scratch_shapes=[
            pltpu.VMEM((NODE, NODE + HALO), BF16),
            pltpu.VMEM((HALO, NODE), BF16),
            pltpu.VMEM((TILES + 1, BLK, BLK), F32),
            pltpu.VMEM((2, 48, BLK, BLK), BF16),
            pltpu.VMEM((NODE, F_IN), BF16),
            pltpu.VMEM((NODE, 2 * F_IN), BF16),
            pltpu.VMEM((HALO, F_IN), BF16),
            pltpu.VMEM((NODE, HID), BF16),
            pltpu.VMEM((HALO, HID), BF16),
            pltpu.VMEM((HID, HALO), BF16),
            pltpu.VMEM((NODE, F_IN), F32),
            pltpu.VMEM((NODE, HID), F32),
            pltpu.VMEM((NODE, HID), BF16),
            pltpu.VMEM((HID, NODE), BF16),
            pltpu.VMEM((HID, NODE), BF16),
            pltpu.VMEM((HID, NODE), BF16),
            pltpu.VMEM((HALO, BLK), F32),
            pltpu.VMEM((HALO, F_IN), BF16),
            pltpu.VMEM((HALO, HID), BF16),
            pltpu.VMEM((HALO, HID), BF16),
            pltpu.VMEM((2 * HID, HID), BF16),
            pltpu.VMEM((PIECES * SLOT, BLK), BF16),
            pltpu.VMEM((PARTS * SLOT, BLK), BF16),
            pltpu.VMEM((PIECES * SLOT, BLK), BF16),
            pltpu.VMEM((SLOT, BLK), F32),
            pltpu.SemaphoreType.DMA((2,)),
            pltpu.SemaphoreType.DMA((3,)),
            pltpu.SemaphoreType.DMA((5,)),
            pltpu.SemaphoreType.DMA((5,)),
            pltpu.SemaphoreType.DMA((2,)),
        ],
        compiler_params=pltpu.CompilerParams(
            collective_id=0, has_side_effects=True, vmem_limit_bytes=62 * 1024 * 1024
        ),
        cost_estimate=pl.CostEstimate(
            flops=20_000_000_000, bytes_accessed=14_000_000, transcendentals=2_000_000
        ),
        name="train_step",
    )(
        nxt, first, part_size,
        features, tile_values, stale_hidden, stale_grads,
        self_one, neigh_one, self_two, neigh_two, send_rows[0], send_count,
        labels.reshape(1, NODE), train_mask.reshape(1, NODE),
    )
    return tuple(outs)


def solution(mesh):
    part = P(("row", "col"))
    return jax.shard_map(
        local,
        mesh=mesh,
        in_specs=(
            part, P(), P(), P(), P(), part, part, part, part, part, part, P(), part, part, part, part,
        ),
        out_specs=(P(), P(), P(), P(), part, part),
        check_vma=False,
    )
```

```python
import jax
import jax.numpy as jnp
from jax import lax
from jax.experimental import pallas as pl
from jax.experimental.pallas import tpu as pltpu
from jax.sharding import PartitionSpec as P

MESH = pl.DeviceIdType.MESH
F32 = jnp.float32
BF16 = jnp.bfloat16
NODE = 2048
HALF = 1024
HALO = 2048
BLK = 128
SLOT = 16
PARTS = 128
COLS = 32
TILES = 192
STAGE = 48
F_IN = 128
HID = 256
CLS = 172
CLSP = 176
CH = 512
NCH = 4
PIECE = 48
SIDE = 16 * PIECE
LOSS_SCALE = 1.0 / 32.0


def dot(a, b):
    return lax.dot_general(a, b, (((1,), (0,)), ((), ())), preferred_element_type=F32)


def dot_nt(a, b):
    return lax.dot_general(a, b, (((1,), (1,)), ((), ())), preferred_element_type=F32)


def at(start, size):
    return pl.ds(pl.multiple_of(start, size), size)


def device(index):
    return (index >> 5, index & 31)


def offset(s):
    k, dx, dy, core = s >> 5, (s >> 3) & 3, (s >> 1) & 3, s & 1
    dz = k ^ dx ^ dy
    return (dx << 5) + (dy << 3) + (dz << 1) + core


def choose(upper, wide):
    width = wide.shape[1] // 2
    cuts = []
    for b in range(width // BLK):
        low = wide[:, b * BLK : (b + 1) * BLK]
        high = wide[:, width + b * BLK : width + (b + 1) * BLK]
        cuts.append(jnp.where(upper, high, low))
    return cuts[0] if len(cuts) == 1 else jnp.concatenate(cuts, axis=1)


def prepare(
    rows_s, cols_s, count_s, size_s, tiles_hbm, feat_hbm, rows_hbm, count_hbm,
    adj, pick, own, send1, upper_ref, recv_ref,
    tbuf, sums, own_wide, rows_ref, count_ref, state, slot_block, tile_sem, load_sem,
):
    me = lax.axis_index("row") * COLS + lax.axis_index("col")
    size = size_s[0]
    used = count_s[0]

    load_rows = pltpu.make_async_copy(rows_hbm, rows_ref, load_sem.at[1])
    load_rows.start()
    load_count = pltpu.make_async_copy(count_hbm, count_ref, load_sem.at[2])
    load_count.start()
    load_own = pltpu.make_async_copy(feat_hbm, own, load_sem.at[0])
    load_own.start()

    def load_tiles(k):
        cut = pl.ds(k * STAGE, STAGE)
        return pltpu.make_async_copy(tiles_hbm.at[cut], tbuf.at[cut], tile_sem.at[k])

    for k in range(TILES // STAGE):
        load_tiles(k).start()

    load_rows.wait()
    load_count.wait()

    part = lax.broadcasted_iota(jnp.int32, (PARTS, BLK), 0)
    is_me = jnp.where(part == me, 1.0, 0.0).astype(BF16)
    counts = count_ref[...].astype(F32)
    in_count = dot(counts.astype(BF16), is_me).astype(BF16)
    out_count = dot(jnp.transpose(counts).astype(BF16), is_me).astype(BF16)
    rows = rows_ref[...]
    high = (rows >> 7).astype(F32).astype(BF16)
    low = (rows & 127).astype(F32).astype(BF16)
    ones = jnp.ones((SLOT, BLK), BF16)

    def build_pick(k, c):
        cut = at(k * CH, CH)
        h = lax.broadcasted_iota(jnp.int32, (CH, PARTS), 0) + k * CH
        q = lax.broadcasted_iota(jnp.int32, (CH, PARTS), 1)
        expand = jnp.where((offset(h >> 4) ^ me) == q, 1.0, 0.0).astype(BF16)
        hs = lax.broadcasted_iota(jnp.int32, (CH, SLOT), 0)
        js = lax.broadcasted_iota(jnp.int32, (CH, SLOT), 1)
        slot_is = (hs & 15) == js
        high_b = dot(jnp.where(slot_is, dot_nt(expand, high), 0.0).astype(BF16), ones)
        low_b = dot(jnp.where(slot_is, dot_nt(expand, low), 0.0).astype(BF16), ones)
        j_of = (h & 15).astype(F32)
        live = j_of < dot(expand, out_count)
        upper = high_b >= 8.0
        upper_ref[cut, :] = jnp.where(upper, 1.0, 0.0).astype(BF16)
        key = jnp.where(upper, high_b - 8.0, high_b)
        key = jnp.where(live & (low_b == q.astype(F32)), key, -1.0)
        for b in range(HALF // BLK):
            pick[cut, b * BLK : (b + 1) * BLK] = jnp.where(key == float(b), 1.0, 0.0).astype(BF16)
        natural = jnp.where((h >> 4) == q, 1.0, 0.0).astype(BF16)
        recv_ref[cut, :] = jnp.where(j_of < dot(natural, in_count), 1.0, 0.0).astype(BF16)
        return c

    lax.fori_loop(0, NCH, build_pick, 0)

    load_own.wait()

    def mask_own(k, c):
        cut = at(k * CH, CH)
        row = lax.broadcasted_iota(jnp.int32, (CH, F_IN), 0) + k * CH
        kept = jnp.where(row < size, own[cut, :].astype(F32), 0.0).astype(BF16)
        own[cut, :] = kept
        own_wide[at((k & 1) * CH, CH), at((k >> 1) * F_IN, F_IN)] = kept
        return c

    lax.fori_loop(0, NCH, mask_own, 0)

    def gather_feats(k, c):
        cut = at(k * CH, CH)
        both_halves = dot(pick[cut, :], own_wide[...])
        upper = upper_ref[cut, :].astype(F32) > 0.0
        send1[cut, :] = choose(upper, both_halves).astype(BF16)
        return c

    lax.fori_loop(0, NCH, gather_feats, 0)

    def clear(i, c):
        adj[at(i * BLK, BLK), :] = jnp.zeros((BLK, NODE + HALO), BF16)
        return c

    lax.fori_loop(0, NODE // BLK, clear, 0)

    def clear_state(i, c):
        state[i] = 0
        return c

    lax.fori_loop(0, 512, clear_state, 0, unroll=8)
    state[512] = 0

    def place(t, c):
        r, col = rows_s[0, t], cols_s[0, t]
        block = r * 32 + col
        known = state[block]
        where = (at(r * BLK, BLK), at(col * BLK, BLK))

        @pl.when(known == 0)
        def _():
            adj[where] = tbuf[t]
            state[block] = 1

        @pl.when(known == 1)
        def _():
            slot = state[512]
            sums[slot] = adj[where].astype(F32) + tbuf[t].astype(F32)
            slot_block[slot] = block
            state[block] = slot + 2
            state[512] = slot + 1

        @pl.when(known > 1)
        def _():
            sums[known - 2] += tbuf[t].astype(F32)

        return c

    for k in range(TILES // STAGE):
        load_tiles(k).wait()
        lax.fori_loop(k * STAGE, jnp.clip(used, k * STAGE, (k + 1) * STAGE), place, 0)

    def settle(slot, c):
        block = slot_block[slot]
        adj[at((block >> 5) * BLK, BLK), at((block & 31) * BLK, BLK)] = sums[slot].astype(BF16)
        return c

    lax.fori_loop(0, state[512], settle, 0)


def step(
    size_ref, stale_hbm, grads_hbm,
    adj, pick, own, send1, upper_ref, recv_ref,
    w1s_ref, w1n_ref, w2s_ref, w2n_ref, labels_ref, mask_ref,
    gs1_ref, gn1_ref, gs2_ref, gn2_ref, fh_hbm, fg_hbm,
    both, agg_wide, halo, two, stale, grads, grad_t, acc1, acc2,
    gl_t, ga_t, gp_t, send2, agg_in, send3, w1, w2, fresh_buf,
    contrib, pair_in, pair_sum, plane_in, z_in, result,
    load_sem, ssem, rsem, local_sem,
):
    my_row = lax.axis_index("row")
    my_col = lax.axis_index("col")
    me = my_row * COLS + my_col
    my_y, my_zc = my_col >> 3, my_col & 7
    my_z, my_core = (my_col >> 1) & 3, my_col & 1
    my_xy = my_row * 4 + my_y
    size = size_ref[0]

    barrier = pltpu.get_barrier_semaphore()

    def greet(i, c):
        pl.semaphore_signal(
            barrier, inc=1, device_id=device(me ^ i), device_id_type=MESH
        )
        return c

    lax.fori_loop(1, PARTS, greet, 0)

    load_grads = pltpu.make_async_copy(grads_hbm, grads, load_sem.at[0])
    load_grads.start()
    load_stale = pltpu.make_async_copy(stale_hbm, stale, load_sem.at[1])
    load_stale.start()

    w1[0:F_IN, :] = w1s_ref[...]
    w1[F_IN : 2 * F_IN, :] = w1n_ref[...]
    w2[...] = jnp.zeros_like(w2)
    w2[0:CLS, 0:HID] = w2s_ref[...]
    w2[0:CLS, HID : 2 * HID] = w2n_ref[...]

    def piece_of(index):
        return at(index * SLOT, SLOT)

    def send_to(src, at_piece, dst, which, d):
        pltpu.make_async_remote_copy(
            src_ref=src.at[piece_of(at_piece)],
            dst_ref=dst.at[piece_of(me)],
            send_sem=ssem.at[which],
            recv_sem=rsem.at[which],
            device_id=device(d),
            device_id_type=MESH,
        ).start()

    def wait_bytes(ref, sem):
        pltpu.make_async_copy(ref, ref, sem).wait()

    pl.semaphore_wait(barrier, PARTS - 1)

    def send_feats(i, c):
        send_to(send1, i, halo, 0, me ^ offset(i))
        return c

    lax.fori_loop(1, PARTS, send_feats, 0)
    halo[piece_of(me), :] = jnp.zeros((SLOT, F_IN), BF16)

    def early_own(k, c):
        cut = at(k * CH, CH)
        both[cut, 0:F_IN] = own[cut, :]
        acc1[cut, :] = dot(adj[cut, 0:NODE], own[...])
        return c

    lax.fori_loop(0, NCH, early_own, 0)

    load_stale.wait()

    def mask_stale(k, c):
        cut = at(k * CH, CH)
        live = recv_ref[cut, :].astype(F32) > 0.0
        for half in range(2):
            lanes = slice(half * BLK, (half + 1) * BLK)
            stale[cut, lanes] = jnp.where(live, stale[cut, lanes].astype(F32), 0.0).astype(BF16)
        return c

    lax.fori_loop(0, NCH, mask_stale, 0)

    def early_stale(k, c):
        cut = at(k * CH, CH)
        acc2[cut, :] = dot(adj[cut, NODE : NODE + HALO], stale[...])
        return c

    lax.fori_loop(0, NCH, early_stale, 0)

    load_grads.wait()

    def order_grads(i, c):
        send3[piece_of(i), :] = grads[piece_of(me ^ offset(i)), :]
        return c

    lax.fori_loop(0, PARTS, order_grads, 0, unroll=8)

    def turn_grads(k, c):
        cut = at(k * CH, CH)
        upper = upper_ref[cut, :].astype(F32) > 0.0
        value = send3[cut, :].astype(F32)
        upper = jnp.concatenate([upper, upper], axis=1)
        grad_t[0, :, cut] = jnp.transpose(jnp.where(upper, 0.0, value).astype(BF16))
        grad_t[1, :, cut] = jnp.transpose(jnp.where(upper, value, 0.0).astype(BF16))
        return c

    lax.fori_loop(0, NCH, turn_grads, 0)

    wait_bytes(halo.at[pl.ds(0, HALO - SLOT)], rsem.at[0])

    def first_agg(k, c):
        cut = at(k * CH, CH)
        agg = (acc1[cut, :] + dot(adj[cut, NODE : NODE + HALO], halo[...])).astype(BF16)
        both[cut, F_IN : 2 * F_IN] = agg
        agg_wide[at((k & 1) * CH, CH), at((k >> 1) * F_IN, F_IN)] = agg
        return c

    lax.fori_loop(0, NCH, first_agg, 0)

    def send_agg(k, c):
        cut = at(k * CH, CH)
        upper = upper_ref[cut, :].astype(F32) > 0.0
        send2[cut, :] = choose(upper, dot(pick[cut, :], agg_wide[...])).astype(BF16)

        def one(i, c2):
            @pl.when(i > 0)
            def _():
                send_to(send2, i, agg_in, 1, me ^ offset(i))

            return c2

        return lax.fori_loop(k * COLS, (k + 1) * COLS, one, c)

    lax.fori_loop(0, NCH, send_agg, 0)
    agg_in[piece_of(me), :] = jnp.zeros((SLOT, F_IN), BF16)

    def first_layer(k, c):
        cut = at(k * CH, CH)
        pre = dot(both[cut, :], w1[...])
        row = lax.broadcasted_iota(jnp.int32, (CH, HID), 0) + k * CH
        act = pre / (1.0 + jnp.exp(-pre))
        two[cut, 0:HID] = jnp.where(row < size, act, 0.0).astype(BF16)
        return c

    lax.fori_loop(0, NCH, first_layer, 0)

    def second_agg(k, c):
        cut = at(k * CH, CH)
        agg = acc2[cut, :] + dot(adj[cut, 0:NODE], two[:, 0:HID])
        two[cut, HID : 2 * HID] = agg.astype(BF16)
        return c

    lax.fori_loop(0, NCH, second_agg, 0)

    gl_t[CLSP:HID, :] = jnp.zeros((HID - CLSP, NODE), BF16)

    def loss_grad(k, c):
        cut = at(k * CH, CH)
        logits = dot_nt(w2[0:CLSP, :], two[cut, :])
        cls = lax.broadcasted_iota(jnp.int32, (CLSP, CH), 0)
        logits = jnp.where(cls < CLS, logits, -jnp.inf)
        expo = jnp.exp(logits - jnp.max(logits, axis=0, keepdims=True))
        total = jnp.sum(expo, axis=0, keepdims=True)
        node = lax.broadcasted_iota(jnp.int32, (1, CH), 1) + k * CH
        weight = jnp.where((node < size) & (mask_ref[:, cut] > 0), LOSS_SCALE, 0.0)
        target = jnp.where(cls == labels_ref[:, cut], 1.0, 0.0)
        gl_t[0:CLSP, cut] = ((expo * (1.0 / total) - target) * weight).astype(BF16)
        return c

    lax.fori_loop(0, NCH, loss_grad, 0)

    w2s = jnp.transpose(w2[:, 0:HID])
    w2n = jnp.transpose(w2[:, HID : 2 * HID])

    def back_agg(k, c):
        cut = at(k * CH, CH)
        ga_t[:, cut] = dot(w2n, gl_t[:, cut]).astype(BF16)
        return c

    lax.fori_loop(0, NCH, back_agg, 0)

    def block_at(dx, k):
        return (my_row ^ dx) * 4 + (my_y ^ dx ^ k)

    def make_spread(k):
        for pair in range(2):
            blocks = [block_at(2 * pair, k), block_at(2 * pair + 1, k)]
            cols = [adj[:, at(NODE + b * BLK, BLK)] for b in blocks]
            spread = jnp.transpose(dot(ga_t[...], jnp.concatenate(cols, axis=1)))
            for b, part in zip(blocks, (spread[0:BLK], spread[BLK : 2 * BLK])):
                cut = at(b * BLK, BLK)
                live = recv_ref[cut, :].astype(F32) > 0.0
                for half in range(2):
                    lanes = slice(half * BLK, (half + 1) * BLK)
                    send3[cut, lanes] = jnp.where(live, part[:, lanes], 0.0).astype(BF16)

    def send_spread(k):
        def one(i, c):
            d = block_at(i & 3, k) * 8 + (my_zc ^ (i >> 2))

            @pl.when(d != me)
            def _():
                send_to(send3, d, fg_hbm, 2, d)

            return c

        lax.fori_loop(0, COLS, one, 0)

    def part_copy(which, src, dst, d):
        pltpu.make_async_remote_copy(
            src_ref=src,
            dst_ref=dst,
            send_sem=ssem.at[which],
            recv_sem=rsem.at[which],
            device_id=device(d),
            device_id_type=MESH,
        ).start()

    mine = at(my_core * SIDE, SIDE)
    other = at((1 - my_core) * SIDE, SIDE)
    home = at(my_core * SIDE + my_xy * PIECE, PIECE)

    def plane_peer(i):
        return me ^ ((i >> 2) << 5) ^ ((i & 3) << 3)

    def plane_index(d):
        return (d >> 5) * 4 + ((d >> 3) & 3)

    def reduce_pair():
        part_copy(3, contrib.at[other], pair_in, me ^ 1)

    def reduce_plane():
        wait_bytes(pair_in, rsem.at[3])
        pair_sum[...] = (contrib[mine, :].astype(F32) + pair_in[...].astype(F32)).astype(BF16)

        def one(i, c):
            d = plane_peer(i)
            part_copy(
                4, pair_sum.at[at(plane_index(d) * PIECE, PIECE)],
                plane_in.at[at(my_xy * PIECE, PIECE)], d,
            )
            return c

        lax.fori_loop(1, 16, one, 0)

    def reduce_z():
        wait_bytes(plane_in.at[pl.ds(0, 15 * PIECE)], rsem.at[4])
        plane_in[at(my_xy * PIECE, PIECE), :] = pair_sum[at(my_xy * PIECE, PIECE), :]
        z_in[at(my_z * PIECE, PIECE), :] = jnp.sum(
            plane_in[...].astype(F32).reshape(16, PIECE, BLK), axis=0
        ).astype(BF16)
        for i in range(1, 4):
            cut = at(my_z * PIECE, PIECE)
            part_copy(5, z_in.at[cut], z_in.at[cut], me ^ (i << 1))

    def return_plane():
        wait_bytes(z_in.at[pl.ds(0, 3 * PIECE)], rsem.at[5])
        result[home, :] = jnp.sum(
            z_in[...].astype(F32).reshape(4, PIECE, BLK), axis=0
        ).astype(BF16)

        def one(i, c):
            part_copy(6, result.at[home], result.at[home], plane_peer(i))
            return c

        lax.fori_loop(1, 16, one, 0)

    def return_pair():
        wait_bytes(result.at[pl.ds(0, 15 * PIECE)], rsem.at[6])
        part_copy(7, result.at[mine], result.at[mine], me ^ 1)

    contrib[...] = jnp.zeros_like(contrib)
    g2 = dot(gl_t[0:CLSP, :], two[...])
    for b in range(4):
        contrib[2 * HID + b * CLSP : 2 * HID + (b + 1) * CLSP, :] = g2[
            :, b * BLK : (b + 1) * BLK
        ].astype(BF16)

    w1_t = jnp.transpose(w1[...])

    def back_first(k, c):
        cut = at(k * CH, CH)
        grad = dot(ga_t[...], adj[:, cut]) + dot(grad_t[k >> 1], pick[:, at((k & 1) * CH, CH)])
        grad = grad + dot(w2s, gl_t[:, cut])
        pre = dot_nt(w1_t, both[cut, :])
        sigma = 1.0 / (1.0 + jnp.exp(-pre))
        slope = sigma * (1.0 + pre * (1.0 - sigma))
        node = lax.broadcasted_iota(jnp.int32, (HID, CH), 1) + k * CH
        gp_t[:, cut] = jnp.where(node < size, grad * slope, 0.0).astype(BF16)
        return c

    make_spread(0)
    send_spread(0)
    lax.fori_loop(0, 2, back_first, 0)
    make_spread(1)
    send_spread(1)
    lax.fori_loop(2, NCH, back_first, 0)

    g1 = dot(gp_t[...], both[...])
    contrib[0:HID, :] = g1[:, 0:F_IN].astype(BF16)
    contrib[HID : 2 * HID, :] = g1[:, F_IN : 2 * F_IN].astype(BF16)
    reduce_pair()
    make_spread(2)
    reduce_plane()
    send_spread(2)
    make_spread(3)
    reduce_z()
    send_spread(3)
    own_spread = pltpu.make_async_copy(
        send3.at[piece_of(me)], fg_hbm.at[piece_of(me)], local_sem.at[0]
    )
    own_spread.start()

    wait_bytes(agg_in.at[pl.ds(0, HALO - SLOT)], rsem.at[1])

    def fresh(k, c):
        cut = at(k * CH, CH)
        pre = dot(halo[cut, :], w1[0:F_IN, :]) + dot(agg_in[cut, :], w1[F_IN : 2 * F_IN, :])
        fresh_buf[cut, :] = (pre / (1.0 + jnp.exp(-pre))).astype(BF16)
        return c

    lax.fori_loop(0, NCH, fresh, 0)
    give_fresh = pltpu.make_async_copy(fresh_buf, fh_hbm, local_sem.at[1])
    give_fresh.start()

    return_plane()
    return_pair()
    wait_bytes(result.at[other], rsem.at[7])

    gs1_ref[...] = jnp.transpose(result[0:HID, :].astype(F32))
    gn1_ref[...] = jnp.transpose(result[HID : 2 * HID, :].astype(F32))
    for b, (dst, half) in enumerate(((gs2_ref, 0), (gs2_ref, 1), (gn2_ref, 0), (gn2_ref, 1))):
        block = result[2 * HID + b * CLSP : 2 * HID + (b + 1) * CLSP, :].astype(F32)
        dst[:, half * BLK : (half + 1) * BLK] = block[0:CLS, :]

    wait_bytes(send1.at[pl.ds(0, HALO - SLOT)], ssem.at[0])
    wait_bytes(send2.at[pl.ds(0, HALO - SLOT)], ssem.at[1])
    wait_bytes(send3.at[pl.ds(0, HALO - SLOT)], ssem.at[2])
    wait_bytes(contrib.at[mine], ssem.at[3])
    wait_bytes(plane_in.at[pl.ds(0, 15 * PIECE)], ssem.at[4])
    wait_bytes(z_in.at[pl.ds(0, 3 * PIECE)], ssem.at[5])
    wait_bytes(result.at[pl.ds(0, 15 * PIECE)], ssem.at[6])
    wait_bytes(result.at[mine], ssem.at[7])
    own_spread.wait()
    give_fresh.wait()
    wait_bytes(fg_hbm.at[pl.ds(0, HALO - SLOT)], rsem.at[2])


def hand_over(*refs):
    held, sems = refs[12:18], refs[18]
    into = [pltpu.make_async_copy(refs[i], held[i], sems.at[i]) for i in range(6)]
    out = [pltpu.make_async_copy(held[i], refs[6 + i], sems.at[6 + i]) for i in range(6)]
    for copy in into[::-1]:
        copy.start()
    for i in range(5, -1, -1):
        into[i].wait()
        out[i].start()
    for copy in out:
        copy.wait()


def local(
    features, self_one, neigh_one, self_two, neigh_two, tile_values, tile_rows, tile_cols,
    tile_count, part_size, send_rows, send_count, labels, train_mask, stale_hidden, stale_grads,
):
    def in_hbm(x):
        return pltpu.with_memory_space_constraint(x, pltpu.HBM)

    smem = pl.BlockSpec(memory_space=pltpu.SMEM)
    vmem = pl.BlockSpec(memory_space=pltpu.VMEM)
    hbm = pl.BlockSpec(memory_space=pltpu.HBM)
    anywhere = pl.BlockSpec(memory_space=pl.ANY)
    packed = pl.pallas_call(
        prepare,
        out_shape=(
            jax.ShapeDtypeStruct((NODE, NODE + HALO), BF16),
            jax.ShapeDtypeStruct((HALO, HALF), BF16),
            jax.ShapeDtypeStruct((NODE, F_IN), BF16),
            jax.ShapeDtypeStruct((HALO, F_IN), BF16),
            jax.ShapeDtypeStruct((HALO, BLK), BF16),
            jax.ShapeDtypeStruct((HALO, BLK), BF16),
        ),
        in_specs=[smem] * 4 + [hbm] * 4,
        out_specs=(vmem,) * 6,
        scratch_shapes=[
            pltpu.VMEM((TILES, BLK, BLK), BF16),
            pltpu.VMEM((TILES // 2, BLK, BLK), F32),
            pltpu.VMEM((HALF, 2 * F_IN), BF16),
            pltpu.VMEM((SLOT, PARTS), jnp.int32),
            pltpu.VMEM((PARTS, PARTS), jnp.int32),
            pltpu.SMEM((520,), jnp.int32),
            pltpu.SMEM((TILES // 2,), jnp.int32),
            pltpu.SemaphoreType.DMA((TILES // STAGE,)),
            pltpu.SemaphoreType.DMA((3,)),
        ],
        compiler_params=pltpu.CompilerParams(vmem_limit_bytes=20 * 1024 * 1024),
        cost_estimate=pl.CostEstimate(
            flops=1_500_000_000, bytes_accessed=8_000_000, transcendentals=0
        ),
        name="prepare",
    )(
        in_hbm(tile_rows), in_hbm(tile_cols), tile_count, part_size,
        *(in_hbm(x) for x in (tile_values, features, send_rows[0].T, send_count)),
    )
    outs = pl.pallas_call(
        step,
        out_shape=(
            jax.ShapeDtypeStruct((F_IN, HID), F32),
            jax.ShapeDtypeStruct((F_IN, HID), F32),
            jax.ShapeDtypeStruct((CLS, HID), F32),
            jax.ShapeDtypeStruct((CLS, HID), F32),
            jax.ShapeDtypeStruct((HALO, HID), BF16),
            jax.ShapeDtypeStruct((HALO, HID), BF16),
        ),
        in_specs=[smem] + [hbm] * 2 + [vmem] * 12,
        out_specs=(vmem,) * 4 + (anywhere,) * 2,
        scratch_shapes=[
            pltpu.VMEM((NODE, 2 * F_IN), BF16),
            pltpu.VMEM((HALF, 2 * F_IN), BF16),
            pltpu.VMEM((HALO, F_IN), BF16),
            pltpu.VMEM((NODE, 2 * HID), BF16),
            pltpu.VMEM((HALO, HID), BF16),
            pltpu.VMEM((HALO, HID), BF16),
            pltpu.VMEM((2, HID, HALO), BF16),
            pltpu.VMEM((NODE, F_IN), F32),
            pltpu.VMEM((NODE, HID), F32),
            pltpu.VMEM((HID, NODE), BF16),
            pltpu.VMEM((HID, NODE), BF16),
            pltpu.VMEM((HID, NODE), BF16),
            pltpu.VMEM((HALO, F_IN), BF16),
            pltpu.VMEM((HALO, F_IN), BF16),
            pltpu.VMEM((HALO, HID), BF16),
            pltpu.VMEM((2 * F_IN, HID), BF16),
            pltpu.VMEM((HID, 2 * HID), BF16),
            pltpu.VMEM((HALO, HID), BF16),
            pltpu.VMEM((2 * SIDE, BLK), BF16),
            pltpu.VMEM((SIDE, BLK), BF16),
            pltpu.VMEM((SIDE, BLK), BF16),
            pltpu.VMEM((SIDE, BLK), BF16),
            pltpu.VMEM((4 * PIECE, BLK), BF16),
            pltpu.VMEM((2 * SIDE, BLK), BF16),
            pltpu.SemaphoreType.DMA((2,)),
            pltpu.SemaphoreType.DMA((8,)),
            pltpu.SemaphoreType.DMA((8,)),
            pltpu.SemaphoreType.DMA((2,)),
        ],
        compiler_params=pltpu.CompilerParams(
            collective_id=0, has_side_effects=True, vmem_limit_bytes=23 * 1024 * 1024
        ),
        cost_estimate=pl.CostEstimate(
            flops=20_000_000_000, bytes_accessed=8_000_000, transcendentals=2_000_000
        ),
        name="train_step",
    )(
        part_size, in_hbm(stale_hidden), in_hbm(stale_grads), *packed,
        self_one, neigh_one, self_two.T, neigh_two.T,
        labels.reshape(1, NODE), train_mask.reshape(1, NODE),
    )
    gs1, gn1, gs2, gn2, fresh_hidden, fresh_grads = pl.pallas_call(
        hand_over,
        out_shape=tuple(jax.ShapeDtypeStruct(o.shape, o.dtype) for o in outs),
        in_specs=[anywhere] * 6,
        out_specs=(anywhere,) * 6,
        scratch_shapes=[pltpu.VMEM(o.shape, o.dtype) for o in outs] + [pltpu.SemaphoreType.DMA((12,))],
        name="hand_over",
    )(*(in_hbm(o) for o in outs))
    return (gs1, gn1, gs2.T, gn2.T, fresh_hidden, fresh_grads)


def solution(mesh):
    part = P(("row", "col"))
    return jax.shard_map(
        local,
        mesh=mesh,
        in_specs=(
            part, P(), P(), P(), P(), part, part, part, part, part, part, P(), part, part, part, part,
        ),
        out_specs=(P(), P(), P(), P(), part, part),
        check_vma=False,
    )
```

```python
import jax
import jax.numpy as jnp
from jax import lax
from jax.experimental import pallas as pl
from jax.experimental.pallas import tpu as pltpu
from jax.sharding import PartitionSpec as P

MESH = pl.DeviceIdType.MESH
F32 = jnp.float32
BF16 = jnp.bfloat16
NODE = 2048
HALF = 1024
HALO = 2048
BLK = 128
SLOT = 16
PARTS = 128
COLS = 32
TILES = 192
STAGE = 48
F_IN = 128
HID = 256
CLS = 172
CLSP = 176
CH = 512
NCH = 4
BIG = 1024
PIECE = 48
SIDE = 16 * PIECE
LOSS_SCALE = 1.0 / 32.0


def dot(a, b):
    return lax.dot_general(a, b, (((1,), (0,)), ((), ())), preferred_element_type=F32)


def dot_nt(a, b):
    return lax.dot_general(a, b, (((1,), (1,)), ((), ())), preferred_element_type=F32)


def at(start, size):
    return pl.ds(pl.multiple_of(start, size), size)


def device(index):
    return (index >> 5, index & 31)


def offset(s):
    k, dx, dy, core = s >> 5, (s >> 3) & 3, (s >> 1) & 3, s & 1
    dz = k ^ dx ^ dy
    return (dx << 5) + (dy << 3) + (dz << 1) + core


def choose(upper, wide):
    width = wide.shape[1] // 2
    cuts = []
    for b in range(width // BLK):
        low = wide[:, b * BLK : (b + 1) * BLK]
        high = wide[:, width + b * BLK : width + (b + 1) * BLK]
        cuts.append(jnp.where(upper, high, low))
    return cuts[0] if len(cuts) == 1 else jnp.concatenate(cuts, axis=1)


def prepare(
    rows_s, cols_s, count_s, size_s, tiles_hbm, feat_hbm, rows_hbm, count_hbm,
    adj, pick, own, send1, upper_ref, recv_ref,
    tbuf, sums, own_wide, rows_ref, count_ref, state, slot_block, tile_sem, load_sem,
):
    me = lax.axis_index("row") * COLS + lax.axis_index("col")
    size = size_s[0]
    used = count_s[0]

    load_rows = pltpu.make_async_copy(rows_hbm, rows_ref, load_sem.at[1])
    load_rows.start()
    load_count = pltpu.make_async_copy(count_hbm, count_ref, load_sem.at[2])
    load_count.start()
    load_own = pltpu.make_async_copy(feat_hbm, own, load_sem.at[0])
    load_own.start()

    def load_tiles(k):
        cut = pl.ds(k * STAGE, STAGE)
        return pltpu.make_async_copy(tiles_hbm.at[cut], tbuf.at[cut], tile_sem.at[k])

    for k in range(TILES // STAGE):
        load_tiles(k).start()

    load_rows.wait()
    load_count.wait()

    part = lax.broadcasted_iota(jnp.int32, (PARTS, BLK), 0)
    is_me = jnp.where(part == me, 1.0, 0.0).astype(BF16)
    counts = count_ref[...].astype(F32)
    in_count = dot(counts.astype(BF16), is_me).astype(BF16)
    out_count = dot(jnp.transpose(counts).astype(BF16), is_me).astype(BF16)
    rows = rows_ref[...]
    high = (rows >> 7).astype(F32).astype(BF16)
    low = (rows & 127).astype(F32).astype(BF16)
    ones = jnp.ones((SLOT, BLK), BF16)

    def build_pick(k, c):
        cut = at(k * CH, CH)
        h = lax.broadcasted_iota(jnp.int32, (CH, PARTS), 0) + k * CH
        q = lax.broadcasted_iota(jnp.int32, (CH, PARTS), 1)
        expand = jnp.where((offset(h >> 4) ^ me) == q, 1.0, 0.0).astype(BF16)
        hs = lax.broadcasted_iota(jnp.int32, (CH, SLOT), 0)
        js = lax.broadcasted_iota(jnp.int32, (CH, SLOT), 1)
        slot_is = (hs & 15) == js
        high_b = dot(jnp.where(slot_is, dot_nt(expand, high), 0.0).astype(BF16), ones)
        low_b = dot(jnp.where(slot_is, dot_nt(expand, low), 0.0).astype(BF16), ones)
        j_of = (h & 15).astype(F32)
        live = j_of < dot(expand, out_count)
        upper = high_b >= 8.0
        upper_ref[cut, :] = jnp.where(upper, 1.0, 0.0).astype(BF16)
        key = jnp.where(upper, high_b - 8.0, high_b)
        key = jnp.where(live & (low_b == q.astype(F32)), key, -1.0)
        for b in range(HALF // BLK):
            pick[cut, b * BLK : (b + 1) * BLK] = jnp.where(key == float(b), 1.0, 0.0).astype(BF16)
        natural = jnp.where((h >> 4) == q, 1.0, 0.0).astype(BF16)
        recv_ref[cut, :] = jnp.where(j_of < dot(natural, in_count), 1.0, 0.0).astype(BF16)
        return c

    lax.fori_loop(0, NCH, build_pick, 0)

    load_own.wait()

    def mask_own(k, c):
        cut = at(k * CH, CH)
        row = lax.broadcasted_iota(jnp.int32, (CH, F_IN), 0) + k * CH
        kept = jnp.where(row < size, own[cut, :].astype(F32), 0.0).astype(BF16)
        own[cut, :] = kept
        own_wide[at((k & 1) * CH, CH), at((k >> 1) * F_IN, F_IN)] = kept
        return c

    lax.fori_loop(0, NCH, mask_own, 0)

    def gather_feats(k, c):
        cut = at(k * CH, CH)
        both_halves = dot(pick[cut, :], own_wide[...])
        upper = upper_ref[cut, :].astype(F32) > 0.0
        send1[cut, :] = choose(upper, both_halves).astype(BF16)
        return c

    lax.fori_loop(0, NCH, gather_feats, 0)

    def clear(i, c):
        adj[at(i * BLK, BLK), :] = jnp.zeros((BLK, NODE + HALO), BF16)
        for j in range(32):
            state[i * 32 + j] = 0
        return c

    lax.fori_loop(0, NODE // BLK, clear, 0)
    state[512] = 0

    def place(t, c):
        r, col = rows_s[0, t], cols_s[0, t]
        block = r * 32 + col
        known = state[block]
        where = (at(r * BLK, BLK), at(col * BLK, BLK))

        @pl.when(known == 0)
        def _():
            adj[where] = tbuf[t]
            state[block] = 1

        @pl.when(known > 0)
        def _():
            @pl.when(known == 1)
            def _():
                slot = state[512]
                sums[slot] = adj[where].astype(F32) + tbuf[t].astype(F32)
                slot_block[slot] = block
                state[block] = slot + 2
                state[512] = slot + 1

            @pl.when(known > 1)
            def _():
                sums[known - 2] += tbuf[t].astype(F32)

        return c

    for k in range(TILES // STAGE):
        load_tiles(k).wait()
        lax.fori_loop(k * STAGE, jnp.clip(used, k * STAGE, (k + 1) * STAGE), place, 0)

    def settle(slot, c):
        block = slot_block[slot]
        adj[at((block >> 5) * BLK, BLK), at((block & 31) * BLK, BLK)] = sums[slot].astype(BF16)
        return c

    lax.fori_loop(0, state[512], settle, 0)


def step(
    size_ref, stale_hbm, grads_hbm,
    adj, pick, own, send1, upper_ref, recv_ref,
    w1s_ref, w1n_ref, w2s_ref, w2n_ref, labels_ref, mask_ref,
    gs1_hbm, gn1_hbm, gs2_hbm, gn2_hbm, fh_hbm, fg_hbm,
    both, agg_wide, halo, two, stale, grads, grad_t, acc1, acc2,
    gl_t, ga_t, gp_t, send2, agg_in, send3, w1, w2, fresh_buf,
    contrib, pair_in, pair_sum, plane_in, z_in, result, gs1_ref, gn1_ref, gs2_ref, gn2_ref,
    load_sem, ssem, rsem, local_sem,
):
    my_row = lax.axis_index("row")
    my_col = lax.axis_index("col")
    me = my_row * COLS + my_col
    my_y, my_zc = my_col >> 3, my_col & 7
    my_z, my_core = (my_col >> 1) & 3, my_col & 1
    my_xy = my_row * 4 + my_y
    size = size_ref[0]

    barrier = pltpu.get_barrier_semaphore()

    def greet(i, c):
        pl.semaphore_signal(
            barrier, inc=1, device_id=device(me ^ i), device_id_type=MESH
        )
        return c

    lax.fori_loop(1, PARTS, greet, 0)

    load_grads = pltpu.make_async_copy(grads_hbm, grads, load_sem.at[0])
    load_grads.start()
    load_stale = pltpu.make_async_copy(stale_hbm, stale, load_sem.at[1])
    load_stale.start()

    w1[0:F_IN, :] = w1s_ref[...]
    w1[F_IN : 2 * F_IN, :] = w1n_ref[...]
    w2[...] = jnp.zeros_like(w2)
    w2[0:CLS, 0:HID] = w2s_ref[...]
    w2[0:CLS, HID : 2 * HID] = w2n_ref[...]

    def piece_of(index):
        return at(index * SLOT, SLOT)

    def send_to(src, at_piece, dst, which, d):
        pltpu.make_async_remote_copy(
            src_ref=src.at[piece_of(at_piece)],
            dst_ref=dst.at[piece_of(me)],
            send_sem=ssem.at[which],
            recv_sem=rsem.at[which],
            device_id=device(d),
            device_id_type=MESH,
        ).start()

    def wait_bytes(ref, sem):
        pltpu.make_async_copy(ref, ref, sem).wait()

    pl.semaphore_wait(barrier, PARTS - 1)

    def send_feats(i, c):
        send_to(send1, i, halo, 0, me ^ offset(i))
        return c

    lax.fori_loop(1, PARTS, send_feats, 0)
    halo[piece_of(me), :] = jnp.zeros((SLOT, F_IN), BF16)

    def early_own(k, c):
        cut = at(k * BIG, BIG)
        both[cut, 0:F_IN] = own[cut, :]
        acc1[cut, :] = dot(adj[cut, 0:NODE], own[...])
        return c

    lax.fori_loop(0, NODE // BIG, early_own, 0)

    load_stale.wait()

    def mask_stale(k, c):
        cut = at(k * CH, CH)
        live = recv_ref[cut, :].astype(F32) > 0.0
        for half in range(2):
            lanes = slice(half * BLK, (half + 1) * BLK)
            stale[cut, lanes] = jnp.where(live, stale[cut, lanes].astype(F32), 0.0).astype(BF16)
        return c

    lax.fori_loop(0, NCH, mask_stale, 0)

    def early_stale(k, c):
        cut = at(k * BIG, BIG)
        acc2[cut, :] = dot(adj[cut, NODE : NODE + HALO], stale[...])
        return c

    lax.fori_loop(0, NODE // BIG, early_stale, 0)

    load_grads.wait()

    def order_grads(i, c):
        send3[piece_of(i), :] = grads[piece_of(me ^ offset(i)), :]
        return c

    lax.fori_loop(0, PARTS, order_grads, 0, unroll=8)

    def turn_grads(k, c):
        cut = at(k * CH, CH)
        upper = upper_ref[cut, :].astype(F32) > 0.0
        value = send3[cut, :].astype(F32)
        upper = jnp.concatenate([upper, upper], axis=1)
        grad_t[0, :, cut] = jnp.transpose(jnp.where(upper, 0.0, value).astype(BF16))
        grad_t[1, :, cut] = jnp.transpose(jnp.where(upper, value, 0.0).astype(BF16))
        return c

    lax.fori_loop(0, NCH, turn_grads, 0)

    wait_bytes(halo.at[pl.ds(0, HALO - SLOT)], rsem.at[0])

    def first_agg(k, c):
        cut = at(k * BIG, BIG)
        agg = (acc1[cut, :] + dot(adj[cut, NODE : NODE + HALO], halo[...])).astype(BF16)
        both[cut, F_IN : 2 * F_IN] = agg
        agg_wide[:, at(k * F_IN, F_IN)] = agg
        return c

    lax.fori_loop(0, NODE // BIG, first_agg, 0)

    def send_agg(k, c):
        cut = at(k * CH, CH)
        upper = upper_ref[cut, :].astype(F32) > 0.0
        send2[cut, :] = choose(upper, dot(pick[cut, :], agg_wide[...])).astype(BF16)

        def one(i, c2):
            @pl.when(i > 0)
            def _():
                send_to(send2, i, agg_in, 1, me ^ offset(i))

            return c2

        return lax.fori_loop(k * COLS, (k + 1) * COLS, one, c)

    lax.fori_loop(0, NCH, send_agg, 0)
    agg_in[piece_of(me), :] = jnp.zeros((SLOT, F_IN), BF16)

    def first_layer(k, c):
        cut = at(k * CH, CH)
        pre = dot(both[cut, :], w1[...])
        row = lax.broadcasted_iota(jnp.int32, (CH, HID), 0) + k * CH
        act = pre / (1.0 + jnp.exp(-pre))
        two[cut, 0:HID] = jnp.where(row < size, act, 0.0).astype(BF16)
        return c

    lax.fori_loop(0, NCH, first_layer, 0)

    def second_agg(k, c):
        cut = at(k * BIG, BIG)
        agg = acc2[cut, :] + dot(adj[cut, 0:NODE], two[:, 0:HID])
        two[cut, HID : 2 * HID] = agg.astype(BF16)
        return c

    lax.fori_loop(0, NODE // BIG, second_agg, 0)

    gl_t[CLSP:HID, :] = jnp.zeros((HID - CLSP, NODE), BF16)

    def loss_grad(k, c):
        cut = at(k * CH, CH)
        logits = dot_nt(w2[0:CLSP, :], two[cut, :])
        cls = lax.broadcasted_iota(jnp.int32, (CLSP, CH), 0)
        logits = jnp.where(cls < CLS, logits, -jnp.inf)
        expo = jnp.exp(logits - jnp.max(logits, axis=0, keepdims=True))
        total = jnp.sum(expo, axis=0, keepdims=True)
        node = lax.broadcasted_iota(jnp.int32, (1, CH), 1) + k * CH
        weight = jnp.where((node < size) & (mask_ref[:, cut] > 0), LOSS_SCALE, 0.0)
        target = jnp.where(cls == labels_ref[:, cut], 1.0, 0.0)
        gl_t[0:CLSP, cut] = ((expo * (1.0 / total) - target) * weight).astype(BF16)
        return c

    lax.fori_loop(0, NCH, loss_grad, 0)

    w2s = jnp.transpose(w2[:, 0:HID])
    w2n = jnp.transpose(w2[:, HID : 2 * HID])

    def back_agg(k, c):
        cut = at(k * CH, CH)
        ga_t[:, cut] = dot(w2n, gl_t[:, cut]).astype(BF16)
        return c

    lax.fori_loop(0, NCH, back_agg, 0)

    def block_at(dx, k):
        return (my_row ^ dx) * 4 + (my_y ^ dx ^ k)

    def make_spread(k):
        for pair in range(2):
            blocks = [block_at(2 * pair, k), block_at(2 * pair + 1, k)]
            cols = [adj[:, at(NODE + b * BLK, BLK)] for b in blocks]
            spread = jnp.transpose(dot(ga_t[...], jnp.concatenate(cols, axis=1)))
            for b, part in zip(blocks, (spread[0:BLK], spread[BLK : 2 * BLK])):
                cut = at(b * BLK, BLK)
                live = recv_ref[cut, :].astype(F32) > 0.0
                for half in range(2):
                    lanes = slice(half * BLK, (half + 1) * BLK)
                    send3[cut, lanes] = jnp.where(live, part[:, lanes], 0.0).astype(BF16)

    def send_spread(k, begin=0, end=COLS):
        def one(i, c):
            d = block_at(i & 3, k) * 8 + (my_zc ^ (i >> 2))

            @pl.when(d != me)
            def _():
                send_to(send3, d, fg_hbm, 2, d)

            return c

        lax.fori_loop(begin, end, one, 0)

    def part_copy(which, src, dst, d):
        pltpu.make_async_remote_copy(
            src_ref=src,
            dst_ref=dst,
            send_sem=ssem.at[which],
            recv_sem=rsem.at[which],
            device_id=device(d),
            device_id_type=MESH,
        ).start()

    mine = at(my_core * SIDE, SIDE)
    other = at((1 - my_core) * SIDE, SIDE)
    home = at(my_core * SIDE + my_xy * PIECE, PIECE)

    def plane_peer(i):
        return me ^ ((i >> 2) << 5) ^ ((i & 3) << 3)

    def plane_index(d):
        return (d >> 5) * 4 + ((d >> 3) & 3)

    def reduce_pair():
        part_copy(3, contrib.at[other], pair_in, me ^ 1)

    def reduce_plane():
        wait_bytes(pair_in, rsem.at[3])
        pair_sum[...] = (contrib[mine, :].astype(F32) + pair_in[...].astype(F32)).astype(BF16)

        def one(i, c):
            d = plane_peer(i)
            part_copy(
                4, pair_sum.at[at(plane_index(d) * PIECE, PIECE)],
                plane_in.at[at(my_xy * PIECE, PIECE)], d,
            )
            return c

        lax.fori_loop(1, 16, one, 0)

    def reduce_z():
        wait_bytes(plane_in.at[pl.ds(0, 15 * PIECE)], rsem.at[4])
        plane_in[at(my_xy * PIECE, PIECE), :] = pair_sum[at(my_xy * PIECE, PIECE), :]
        z_in[at(my_z * PIECE, PIECE), :] = jnp.sum(
            plane_in[...].astype(F32).reshape(16, PIECE, BLK), axis=0
        ).astype(BF16)
        for i in range(1, 4):
            cut = at(my_z * PIECE, PIECE)
            part_copy(5, z_in.at[cut], z_in.at[cut], me ^ (i << 1))

    def return_plane():
        wait_bytes(z_in.at[pl.ds(0, 3 * PIECE)], rsem.at[5])
        result[home, :] = jnp.sum(
            z_in[...].astype(F32).reshape(4, PIECE, BLK), axis=0
        ).astype(BF16)

        def one(i, c):
            part_copy(6, result.at[home], result.at[home], plane_peer(i))
            return c

        lax.fori_loop(1, 16, one, 0)

    def return_pair():
        wait_bytes(result.at[pl.ds(0, 15 * PIECE)], rsem.at[6])
        part_copy(7, result.at[mine], result.at[mine], me ^ 1)

    contrib[...] = jnp.zeros_like(contrib)
    g2 = dot(gl_t[0:CLSP, :], two[...])
    for b in range(4):
        contrib[2 * HID + b * CLSP : 2 * HID + (b + 1) * CLSP, :] = g2[
            :, b * BLK : (b + 1) * BLK
        ].astype(BF16)

    w1_t = jnp.transpose(w1[...])

    def back_first(k, c):
        cut = at(k * CH, CH)
        grad = dot(ga_t[...], adj[:, cut]) + dot(grad_t[k >> 1], pick[:, at((k & 1) * CH, CH)])
        grad = grad + dot(w2s, gl_t[:, cut])
        pre = dot_nt(w1_t, both[cut, :])
        sigma = 1.0 / (1.0 + jnp.exp(-pre))
        slope = sigma * (1.0 + pre * (1.0 - sigma))
        node = lax.broadcasted_iota(jnp.int32, (HID, CH), 1) + k * CH
        gp_t[:, cut] = jnp.where(node < size, grad * slope, 0.0).astype(BF16)
        return c

    for k in range(3):
        make_spread(k)
        send_spread(k)
    lax.fori_loop(0, NCH, back_first, 0)

    g1 = dot(gp_t[...], both[...])
    contrib[0:HID, :] = g1[:, 0:F_IN].astype(BF16)
    contrib[HID : 2 * HID, :] = g1[:, F_IN : 2 * F_IN].astype(BF16)
    reduce_pair()
    make_spread(3)
    reduce_plane()
    send_spread(3)
    reduce_z()
    wait_bytes(agg_in.at[pl.ds(0, HALO - SLOT)], rsem.at[1])

    def fresh(k, c):
        cut = at(k * CH, CH)
        pre = dot(halo[cut, :], w1[0:F_IN, :]) + dot(agg_in[cut, :], w1[F_IN : 2 * F_IN, :])
        fresh_buf[cut, :] = (pre / (1.0 + jnp.exp(-pre))).astype(BF16)
        return c

    lax.fori_loop(0, NCH, fresh, 0)
    give_fresh = pltpu.make_async_copy(fresh_buf, fh_hbm, local_sem.at[1])
    give_fresh.start()

    return_plane()
    own_spread = pltpu.make_async_copy(
        send3.at[piece_of(me)], fg_hbm.at[piece_of(me)], local_sem.at[0]
    )
    own_spread.start()

    return_pair()
    wait_bytes(result.at[other], rsem.at[7])

    gs1_ref[...] = jnp.transpose(result[0:HID, :].astype(F32))
    gn1_ref[...] = jnp.transpose(result[HID : 2 * HID, :].astype(F32))
    for b, (dst, half) in enumerate(((gs2_ref, 0), (gs2_ref, 1), (gn2_ref, 0), (gn2_ref, 1))):
        block = result[2 * HID + b * CLSP : 2 * HID + (b + 1) * CLSP, :].astype(F32)
        dst[:, half * BLK : (half + 1) * BLK] = block[0:CLS, :]
    gives = [
        pltpu.make_async_copy(src, dst, local_sem.at[2 + i])
        for i, (src, dst) in enumerate(
            ((gs1_ref, gs1_hbm), (gn1_ref, gn1_hbm), (gs2_ref, gs2_hbm), (gn2_ref, gn2_hbm))
        )
    ]
    for give in gives:
        give.start()

    wait_bytes(send1.at[pl.ds(0, HALO - SLOT)], ssem.at[0])
    wait_bytes(send2.at[pl.ds(0, HALO - SLOT)], ssem.at[1])
    wait_bytes(send3.at[pl.ds(0, HALO - SLOT)], ssem.at[2])
    wait_bytes(contrib.at[mine], ssem.at[3])
    wait_bytes(plane_in.at[pl.ds(0, 15 * PIECE)], ssem.at[4])
    wait_bytes(z_in.at[pl.ds(0, 3 * PIECE)], ssem.at[5])
    wait_bytes(result.at[pl.ds(0, 15 * PIECE)], ssem.at[6])
    wait_bytes(result.at[mine], ssem.at[7])
    own_spread.wait()
    give_fresh.wait()
    for give in gives:
        give.wait()
    wait_bytes(fg_hbm.at[pl.ds(0, HALO - SLOT)], rsem.at[2])


def hand_over(*refs):
    held, sems = refs[12:18], refs[18]
    into = [pltpu.make_async_copy(refs[i], held[i], sems.at[i]) for i in range(6)]
    out = [pltpu.make_async_copy(held[i], refs[6 + i], sems.at[6 + i]) for i in range(6)]
    for copy in into[::-1]:
        copy.start()
    for i in range(5, -1, -1):
        into[i].wait()
        out[i].start()
    for copy in out:
        copy.wait()


def local(
    features, self_one, neigh_one, self_two, neigh_two, tile_values, tile_rows, tile_cols,
    tile_count, part_size, send_rows, send_count, labels, train_mask, stale_hidden, stale_grads,
):
    def in_hbm(x):
        return pltpu.with_memory_space_constraint(x, pltpu.HBM)

    smem = pl.BlockSpec(memory_space=pltpu.SMEM)
    vmem = pl.BlockSpec(memory_space=pltpu.VMEM)
    hbm = pl.BlockSpec(memory_space=pltpu.HBM)
    packed = pl.pallas_call(
        prepare,
        out_shape=(
            jax.ShapeDtypeStruct((NODE, NODE + HALO), BF16),
            jax.ShapeDtypeStruct((HALO, HALF), BF16),
            jax.ShapeDtypeStruct((NODE, F_IN), BF16),
            jax.ShapeDtypeStruct((HALO, F_IN), BF16),
            jax.ShapeDtypeStruct((HALO, BLK), BF16),
            jax.ShapeDtypeStruct((HALO, BLK), BF16),
        ),
        in_specs=[smem] * 4 + [hbm] * 4,
        out_specs=(vmem,) * 6,
        scratch_shapes=[
            pltpu.VMEM((TILES, BLK, BLK), BF16),
            pltpu.VMEM((TILES // 2, BLK, BLK), F32),
            pltpu.VMEM((HALF, 2 * F_IN), BF16),
            pltpu.VMEM((SLOT, PARTS), jnp.int32),
            pltpu.VMEM((PARTS, PARTS), jnp.int32),
            pltpu.SMEM((520,), jnp.int32),
            pltpu.SMEM((TILES // 2,), jnp.int32),
            pltpu.SemaphoreType.DMA((TILES // STAGE,)),
            pltpu.SemaphoreType.DMA((3,)),
        ],
        compiler_params=pltpu.CompilerParams(vmem_limit_bytes=20 * 1024 * 1024),
        cost_estimate=pl.CostEstimate(
            flops=1_500_000_000, bytes_accessed=8_000_000, transcendentals=0
        ),
        name="prepare",
    )(
        in_hbm(tile_rows), in_hbm(tile_cols), tile_count, part_size,
        *(in_hbm(x) for x in (tile_values, features, send_rows[0].T, send_count)),
    )
    outs = pl.pallas_call(
        step,
        out_shape=(
            pltpu.HBM((F_IN, HID), F32),
            pltpu.HBM((F_IN, HID), F32),
            pltpu.HBM((CLS, HID), F32),
            pltpu.HBM((CLS, HID), F32),
            pltpu.HBM((HALO, HID), BF16),
            pltpu.HBM((HALO, HID), BF16),
        ),
        in_specs=[smem] + [hbm] * 2 + [vmem] * 12,
        out_specs=(hbm,) * 6,
        scratch_shapes=[
            pltpu.VMEM((NODE, 2 * F_IN), BF16),
            pltpu.VMEM((HALF, 2 * F_IN), BF16),
            pltpu.VMEM((HALO, F_IN), BF16),
            pltpu.VMEM((NODE, 2 * HID), BF16),
            pltpu.VMEM((HALO, HID), BF16),
            pltpu.VMEM((HALO, HID), BF16),
            pltpu.VMEM((2, HID, HALO), BF16),
            pltpu.VMEM((NODE, F_IN), F32),
            pltpu.VMEM((NODE, HID), F32),
            pltpu.VMEM((HID, NODE), BF16),
            pltpu.VMEM((HID, NODE), BF16),
            pltpu.VMEM((HID, NODE), BF16),
            pltpu.VMEM((HALO, F_IN), BF16),
            pltpu.VMEM((HALO, F_IN), BF16),
            pltpu.VMEM((HALO, HID), BF16),
            pltpu.VMEM((2 * F_IN, HID), BF16),
            pltpu.VMEM((HID, 2 * HID), BF16),
            pltpu.VMEM((HALO, HID), BF16),
            pltpu.VMEM((2 * SIDE, BLK), BF16),
            pltpu.VMEM((SIDE, BLK), BF16),
            pltpu.VMEM((SIDE, BLK), BF16),
            pltpu.VMEM((SIDE, BLK), BF16),
            pltpu.VMEM((4 * PIECE, BLK), BF16),
            pltpu.VMEM((2 * SIDE, BLK), BF16),
            pltpu.VMEM((F_IN, HID), F32),
            pltpu.VMEM((F_IN, HID), F32),
            pltpu.VMEM((CLS, HID), F32),
            pltpu.VMEM((CLS, HID), F32),
            pltpu.SemaphoreType.DMA((2,)),
            pltpu.SemaphoreType.DMA((8,)),
            pltpu.SemaphoreType.DMA((8,)),
            pltpu.SemaphoreType.DMA((6,)),
        ],
        compiler_params=pltpu.CompilerParams(
            collective_id=0, has_side_effects=True, vmem_limit_bytes=25 * 1024 * 1024
        ),
        cost_estimate=pl.CostEstimate(
            flops=20_000_000_000, bytes_accessed=8_000_000, transcendentals=2_000_000
        ),
        name="train_step",
    )(
        part_size, in_hbm(stale_hidden), in_hbm(stale_grads), *packed,
        self_one, neigh_one, self_two.T, neigh_two.T,
        labels.reshape(1, NODE), train_mask.reshape(1, NODE),
    )
    gs1, gn1, gs2, gn2, fresh_hidden, fresh_grads = pl.pallas_call(
        hand_over,
        out_shape=tuple(jax.ShapeDtypeStruct(o.shape, o.dtype) for o in outs),
        in_specs=[hbm] * 6,
        out_specs=(hbm,) * 6,
        scratch_shapes=[pltpu.VMEM(o.shape, o.dtype) for o in outs] + [pltpu.SemaphoreType.DMA((12,))],
        name="hand_over",
    )(*outs)
    return (gs1, gn1, gs2.T, gn2.T, fresh_hidden, fresh_grads)


def solution(mesh):
    part = P(("row", "col"))
    return jax.shard_map(
        local,
        mesh=mesh,
        in_specs=(
            part, P(), P(), P(), P(), part, part, part, part, part, part, P(), part, part, part, part,
        ),
        out_specs=(P(), P(), P(), P(), part, part),
        check_vma=False,
    )
```

```python
import jax
import jax.numpy as jnp
from jax import lax
from jax.experimental import pallas as pl
from jax.experimental.pallas import tpu as pltpu
from jax.sharding import PartitionSpec as P

MESH = pl.DeviceIdType.MESH
F32 = jnp.float32
BF16 = jnp.bfloat16
NODE = 2048
HALF = 1024
HALO = 2048
BLK = 128
SLOT = 16
PARTS = 128
COLS = 32
TILES = 192
STAGE = 48
F_IN = 128
HID = 256
CLS = 172
CLSP = 176
CH = 512
NCH = 4
BIG = 1024
PIECE = 48
SIDE = 16 * PIECE
LOSS_SCALE = 1.0 / 32.0


def dot(a, b):
    return lax.dot_general(a, b, (((1,), (0,)), ((), ())), preferred_element_type=F32)


def dot_nt(a, b):
    return lax.dot_general(a, b, (((1,), (1,)), ((), ())), preferred_element_type=F32)


def at(start, size):
    return pl.ds(pl.multiple_of(start, size), size)


def device(index):
    return (index >> 5, index & 31)


def offset(s):
    k, dx, dy, core = s >> 5, (s >> 3) & 3, (s >> 1) & 3, s & 1
    dz = k ^ dx ^ dy
    return (dx << 5) + (dy << 3) + (dz << 1) + core


def choose(upper, wide):
    width = wide.shape[1] // 2
    cuts = []
    for b in range(width // BLK):
        low = wide[:, b * BLK : (b + 1) * BLK]
        high = wide[:, width + b * BLK : width + (b + 1) * BLK]
        cuts.append(jnp.where(upper, high, low))
    return cuts[0] if len(cuts) == 1 else jnp.concatenate(cuts, axis=1)


def prepare(
    rows_s, cols_s, count_s, size_s, tiles_hbm, feat_hbm, rows_hbm, count_hbm,
    adj, pick, own, send1, upper_ref, in_count,
    tbuf, sums, own_wide, rows_ref, count_ref, state, slot_block, tile_sem, load_sem,
):
    me = lax.axis_index("row") * COLS + lax.axis_index("col")
    size = size_s[0]
    used = count_s[0]

    load_rows = pltpu.make_async_copy(rows_hbm, rows_ref, load_sem.at[1])
    load_rows.start()
    load_count = pltpu.make_async_copy(count_hbm, count_ref, load_sem.at[2])
    load_count.start()
    load_own = pltpu.make_async_copy(feat_hbm, own, load_sem.at[0])
    load_own.start()

    def load_tiles(k):
        cut = pl.ds(k * STAGE, STAGE)
        return pltpu.make_async_copy(tiles_hbm.at[cut], tbuf.at[cut], tile_sem.at[k])

    for k in range(TILES // STAGE):
        load_tiles(k).start()

    load_rows.wait()
    load_count.wait()

    part = lax.broadcasted_iota(jnp.int32, (PARTS, BLK), 0)
    is_me = jnp.where(part == me, 1.0, 0.0).astype(BF16)
    counts = count_ref[...].astype(F32)
    in_count[...] = dot(counts.astype(BF16), is_me).astype(BF16)
    out_count = dot(jnp.transpose(counts).astype(BF16), is_me).astype(BF16)
    rows = rows_ref[...]
    high = (rows >> 7).astype(F32).astype(BF16)
    low = (rows & 127).astype(F32).astype(BF16)
    ones = jnp.ones((SLOT, BLK), BF16)

    def build_pick(k, c):
        cut = at(k * CH, CH)
        h = lax.broadcasted_iota(jnp.int32, (CH, PARTS), 0) + k * CH
        q = lax.broadcasted_iota(jnp.int32, (CH, PARTS), 1)
        expand = jnp.where((offset(h >> 4) ^ me) == q, 1.0, 0.0).astype(BF16)
        hs = lax.broadcasted_iota(jnp.int32, (CH, SLOT), 0)
        js = lax.broadcasted_iota(jnp.int32, (CH, SLOT), 1)
        slot_is = (hs & 15) == js
        high_b = dot(jnp.where(slot_is, dot_nt(expand, high), 0.0).astype(BF16), ones)
        low_b = dot(jnp.where(slot_is, dot_nt(expand, low), 0.0).astype(BF16), ones)
        j_of = (h & 15).astype(F32)
        live = j_of < dot(expand, out_count)
        upper = high_b >= 8.0
        upper_ref[cut, :] = jnp.where(upper, 1.0, 0.0).astype(BF16)
        key = jnp.where(upper, high_b - 8.0, high_b)
        key = jnp.where(live & (low_b == q.astype(F32)), key, -1.0)
        for b in range(HALF // BLK):
            pick[cut, b * BLK : (b + 1) * BLK] = jnp.where(key == float(b), 1.0, 0.0).astype(BF16)
        return c

    lax.fori_loop(0, NCH, build_pick, 0)

    load_own.wait()

    def mask_own(k, c):
        cut = at(k * CH, CH)
        row = lax.broadcasted_iota(jnp.int32, (CH, F_IN), 0) + k * CH
        kept = jnp.where(row < size, own[cut, :].astype(F32), 0.0).astype(BF16)
        own[cut, :] = kept
        own_wide[at((k & 1) * CH, CH), at((k >> 1) * F_IN, F_IN)] = kept
        return c

    lax.fori_loop(0, NCH, mask_own, 0)

    def gather_feats(k, c):
        cut = at(k * CH, CH)
        both_halves = dot(pick[cut, :], own_wide[...])
        upper = upper_ref[cut, :].astype(F32) > 0.0
        send1[cut, :] = choose(upper, both_halves).astype(BF16)
        return c

    lax.fori_loop(0, NCH, gather_feats, 0)

    def clear(i, c):
        adj[at(i * BLK, BLK), :] = jnp.zeros((BLK, NODE + HALO), BF16)
        for j in range(32):
            state[i * 32 + j] = 0
        return c

    lax.fori_loop(0, NODE // BLK, clear, 0)
    state[512] = 0

    def place(t, c):
        r, col = rows_s[0, t], cols_s[0, t]
        block = r * 32 + col
        known = state[block]
        where = (at(r * BLK, BLK), at(col * BLK, BLK))

        @pl.when(known == 0)
        def _():
            adj[where] = tbuf[t]
            state[block] = 1

        @pl.when(known > 0)
        def _():
            @pl.when(known == 1)
            def _():
                slot = state[512]
                sums[slot] = adj[where].astype(F32) + tbuf[t].astype(F32)
                slot_block[slot] = block
                state[block] = slot + 2
                state[512] = slot + 1

            @pl.when(known > 1)
            def _():
                sums[known - 2] += tbuf[t].astype(F32)

        return c

    for k in range(TILES // STAGE):
        load_tiles(k).wait()
        start = k * STAGE
        here = jnp.clip(used - start, 0, STAGE)

        def place_two(i, c, start=start):
            t = start + 2 * i
            r0, c0, r1, c1 = rows_s[0, t], cols_s[0, t], rows_s[0, t + 1], cols_s[0, t + 1]
            first, second = r0 * 32 + c0, r1 * 32 + c1
            fresh = (state[first] == 0) & (state[second] == 0) & (first != second)

            @pl.when(fresh)
            def _():
                adj[at(r0 * BLK, BLK), at(c0 * BLK, BLK)] = tbuf[t]
                adj[at(r1 * BLK, BLK), at(c1 * BLK, BLK)] = tbuf[t + 1]
                state[first] = 1
                state[second] = 1

            @pl.when(jnp.logical_not(fresh))
            def _():
                place(t, 0)
                place(t + 1, 0)

            return c

        lax.fori_loop(0, here >> 1, place_two, 0)

        @pl.when((here & 1) == 1)
        def _(start=start, here=here):
            place(start + here - 1, 0)

    def settle(slot, c):
        block = slot_block[slot]
        adj[at((block >> 5) * BLK, BLK), at((block & 31) * BLK, BLK)] = sums[slot].astype(BF16)
        return c

    lax.fori_loop(0, state[512], settle, 0)


def step(
    size_ref, stale_hbm, grads_hbm,
    adj, pick, own, send1, upper_ref, in_count,
    w1s_ref, w1n_ref, w2s_ref, w2n_ref, labels_ref, mask_ref,
    gs1_hbm, gn1_hbm, gs2_hbm, gn2_hbm, fh_hbm, fg_hbm,
    recv_ref, both, agg_wide, halo, two, stale, grads, grad_t, acc1, acc2, acc3, w2_t, w1_t,
    gl_t, ga_t, gp_t, send2, agg_in, send3, w1, w2,
    contrib, pair_in, pair_sum, plane_in, z_in, result, gs1_ref, gn1_ref, gs2_ref, gn2_ref,
    load_sem, ssem, rsem, local_sem,
):
    my_row = lax.axis_index("row")
    my_col = lax.axis_index("col")
    me = my_row * COLS + my_col
    my_y, my_zc = my_col >> 3, my_col & 7
    my_z, my_core = (my_col >> 1) & 3, my_col & 1
    my_xy = my_row * 4 + my_y
    size = size_ref[0]

    barrier = pltpu.get_barrier_semaphore()

    def greet(i, c):
        pl.semaphore_signal(
            barrier, inc=1, device_id=device(me ^ i), device_id_type=MESH
        )
        return c

    lax.fori_loop(1, PARTS, greet, 0)

    load_grads = pltpu.make_async_copy(grads_hbm, grads, load_sem.at[0])
    load_grads.start()
    load_stale = pltpu.make_async_copy(stale_hbm, stale, load_sem.at[1])
    load_stale.start()

    w1[0:F_IN, :] = w1s_ref[...]
    w1[F_IN : 2 * F_IN, :] = w1n_ref[...]
    w2[...] = jnp.zeros_like(w2)
    w2[0:CLS, 0:HID] = w2s_ref[...]
    w2[0:CLS, HID : 2 * HID] = w2n_ref[...]

    def piece_of(index):
        return at(index * SLOT, SLOT)

    def send_to(src, at_piece, dst, which, d):
        pltpu.make_async_remote_copy(
            src_ref=src.at[piece_of(at_piece)],
            dst_ref=dst.at[piece_of(me)],
            send_sem=ssem.at[which],
            recv_sem=rsem.at[which],
            device_id=device(d),
            device_id_type=MESH,
        ).start()

    def wait_bytes(ref, sem):
        pltpu.make_async_copy(ref, ref, sem).wait()

    pl.semaphore_wait(barrier, PARTS - 1)

    def send_feats(i, c):
        send_to(send1, i, halo, 0, me ^ offset(i))
        return c

    lax.fori_loop(1, PARTS, send_feats, 0)
    halo[piece_of(me), :] = jnp.zeros((SLOT, F_IN), BF16)

    def early_own(k, c):
        cut = at(k * BIG, BIG)
        both[cut, 0:F_IN] = own[cut, :]
        acc1[cut, :] = dot(adj[cut, 0:NODE], own[...])
        return c

    lax.fori_loop(0, NODE // BIG, early_own, 0)

    load_stale.wait()

    def mask_stale(k, c):
        cut = at(k * CH, CH)
        h = lax.broadcasted_iota(jnp.int32, (CH, PARTS), 0) + k * CH
        q = lax.broadcasted_iota(jnp.int32, (CH, PARTS), 1)
        natural = jnp.where((h >> 4) == q, 1.0, 0.0).astype(BF16)
        counted = dot(natural, in_count[...])
        recv_ref[cut, :] = jnp.where((h & 15).astype(F32) < counted, 1.0, 0.0).astype(BF16)
        live = recv_ref[cut, :].astype(F32) > 0.0
        for half in range(2):
            lanes = slice(half * BLK, (half + 1) * BLK)
            stale[cut, lanes] = jnp.where(live, stale[cut, lanes].astype(F32), 0.0).astype(BF16)
        return c

    lax.fori_loop(0, NCH, mask_stale, 0)

    def early_stale(k, c):
        cut = at(k * BIG, BIG)
        acc2[cut, :] = dot(adj[cut, NODE : NODE + HALO], stale[...])
        return c

    lax.fori_loop(0, NODE // BIG, early_stale, 0)

    load_grads.wait()

    def order_grads(i, c):
        send3[piece_of(i), :] = grads[piece_of(me ^ offset(i)), :]
        return c

    lax.fori_loop(0, PARTS, order_grads, 0, unroll=8)

    def turn_grads(k, c):
        cut = at(k * CH, CH)
        upper = upper_ref[cut, :].astype(F32) > 0.0
        value = send3[cut, :].astype(F32)
        upper = jnp.concatenate([upper, upper], axis=1)
        grad_t[0, :, cut] = jnp.transpose(jnp.where(upper, 0.0, value).astype(BF16))
        grad_t[1, :, cut] = jnp.transpose(jnp.where(upper, value, 0.0).astype(BF16))
        return c

    lax.fori_loop(0, NCH, turn_grads, 0)

    def scatter(k, c):
        acc3[:, at(k * CH, CH)] = dot(grad_t[k >> 1], pick[:, at((k & 1) * CH, CH)])
        return c

    lax.fori_loop(0, NCH, scatter, 0)
    w2_t[:, 0:HID] = jnp.transpose(w2[:, 0:HID])
    w2_t[:, HID : 2 * HID] = jnp.transpose(w2[:, HID : 2 * HID])
    w1_t[...] = jnp.transpose(w1[...])

    wait_bytes(halo.at[pl.ds(0, HALO - SLOT)], rsem.at[0])

    def first_agg(k, c):
        cut = at(k * BIG, BIG)
        agg = (acc1[cut, :] + dot(adj[cut, NODE : NODE + HALO], halo[...])).astype(BF16)
        both[cut, F_IN : 2 * F_IN] = agg
        agg_wide[:, at(k * F_IN, F_IN)] = agg
        return c

    lax.fori_loop(0, NODE // BIG, first_agg, 0)

    def send_agg(k, c):
        cut = at(k * CH, CH)
        upper = upper_ref[cut, :].astype(F32) > 0.0
        send2[cut, :] = choose(upper, dot(pick[cut, :], agg_wide[...])).astype(BF16)

        def one(i, c2):
            @pl.when(i > 0)
            def _():
                send_to(send2, i, agg_in, 1, me ^ offset(i))

            return c2

        return lax.fori_loop(k * COLS, (k + 1) * COLS, one, c)

    lax.fori_loop(0, NCH, send_agg, 0)
    agg_in[piece_of(me), :] = jnp.zeros((SLOT, F_IN), BF16)

    def first_layer(k, c):
        cut = at(k * CH, CH)
        pre = dot(both[cut, :], w1[...])
        row = lax.broadcasted_iota(jnp.int32, (CH, HID), 0) + k * CH
        act = pre / (1.0 + jnp.exp(-pre))
        two[cut, 0:HID] = jnp.where(row < size, act, 0.0).astype(BF16)
        return c

    lax.fori_loop(0, NCH, first_layer, 0)

    def second_agg(k, c):
        cut = at(k * BIG, BIG)
        agg = acc2[cut, :] + dot(adj[cut, 0:NODE], two[:, 0:HID])
        two[cut, HID : 2 * HID] = agg.astype(BF16)
        return c

    lax.fori_loop(0, NODE // BIG, second_agg, 0)

    gl_t[CLSP:HID, :] = jnp.zeros((HID - CLSP, NODE), BF16)

    def loss_grad(k, c):
        cut = at(k * CH, CH)
        logits = dot_nt(w2[0:CLSP, :], two[cut, :])
        cls = lax.broadcasted_iota(jnp.int32, (CLSP, CH), 0)
        logits = jnp.where(cls < CLS, logits, -jnp.inf)
        expo = jnp.exp(logits - jnp.max(logits, axis=0, keepdims=True))
        total = jnp.sum(expo, axis=0, keepdims=True)
        node = lax.broadcasted_iota(jnp.int32, (1, CH), 1) + k * CH
        weight = jnp.where((node < size) & (mask_ref[:, cut] > 0), LOSS_SCALE, 0.0)
        target = jnp.where(cls == labels_ref[:, cut], 1.0, 0.0)
        gl_t[0:CLSP, cut] = ((expo * (1.0 / total) - target) * weight).astype(BF16)
        return c

    lax.fori_loop(0, NCH, loss_grad, 0)

    def back_agg(k, c):
        cut = at(k * CH, CH)
        ga_t[:, cut] = dot(w2_t[:, HID : 2 * HID], gl_t[:, cut]).astype(BF16)
        return c

    lax.fori_loop(0, NCH, back_agg, 0)

    def block_at(dx, k):
        return (my_row ^ dx) * 4 + (my_y ^ dx ^ k)

    def make_spread(k):
        for pair in range(2):
            blocks = [block_at(2 * pair, k), block_at(2 * pair + 1, k)]
            cols = [adj[:, at(NODE + b * BLK, BLK)] for b in blocks]
            spread = jnp.transpose(dot(ga_t[...], jnp.concatenate(cols, axis=1)))
            for b, part in zip(blocks, (spread[0:BLK], spread[BLK : 2 * BLK])):
                cut = at(b * BLK, BLK)
                live = recv_ref[cut, :].astype(F32) > 0.0
                for half in range(2):
                    lanes = slice(half * BLK, (half + 1) * BLK)
                    send3[cut, lanes] = jnp.where(live, part[:, lanes], 0.0).astype(BF16)

    def send_spread(k, begin=0, end=COLS):
        def one(i, c):
            d = block_at(i & 3, k) * 8 + (my_zc ^ (i >> 2))

            @pl.when(d != me)
            def _():
                send_to(send3, d, fg_hbm, 2, d)

            return c

        lax.fori_loop(begin, end, one, 0)

    def part_copy(which, src, dst, d):
        pltpu.make_async_remote_copy(
            src_ref=src,
            dst_ref=dst,
            send_sem=ssem.at[which],
            recv_sem=rsem.at[which],
            device_id=device(d),
            device_id_type=MESH,
        ).start()

    mine = at(my_core * SIDE, SIDE)
    other = at((1 - my_core) * SIDE, SIDE)
    home = at(my_core * SIDE + my_xy * PIECE, PIECE)

    def plane_peer(i):
        return me ^ ((i >> 2) << 5) ^ ((i & 3) << 3)

    def plane_index(d):
        return (d >> 5) * 4 + ((d >> 3) & 3)

    def reduce_pair():
        part_copy(3, contrib.at[other], pair_in, me ^ 1)

    def reduce_plane():
        wait_bytes(pair_in, rsem.at[3])
        pair_sum[...] = (contrib[mine, :].astype(F32) + pair_in[...].astype(F32)).astype(BF16)

        def one(i, c):
            d = plane_peer(i)
            part_copy(
                4, pair_sum.at[at(plane_index(d) * PIECE, PIECE)],
                plane_in.at[at(my_xy * PIECE, PIECE)], d,
            )
            return c

        lax.fori_loop(1, 16, one, 0)

    def reduce_z():
        wait_bytes(plane_in.at[pl.ds(0, 15 * PIECE)], rsem.at[4])
        plane_in[at(my_xy * PIECE, PIECE), :] = pair_sum[at(my_xy * PIECE, PIECE), :]
        z_in[at(my_z * PIECE, PIECE), :] = jnp.sum(
            plane_in[...].astype(F32).reshape(16, PIECE, BLK), axis=0
        ).astype(BF16)
        for i in range(1, 4):
            cut = at(my_z * PIECE, PIECE)
            part_copy(5, z_in.at[cut], z_in.at[cut], me ^ (i << 1))

    def return_plane():
        wait_bytes(z_in.at[pl.ds(0, 3 * PIECE)], rsem.at[5])
        result[home, :] = jnp.sum(
            z_in[...].astype(F32).reshape(4, PIECE, BLK), axis=0
        ).astype(BF16)

        def one(i, c):
            part_copy(6, result.at[home], result.at[home], plane_peer(i))
            return c

        lax.fori_loop(1, 16, one, 0)

    def return_pair():
        wait_bytes(result.at[pl.ds(0, 15 * PIECE)], rsem.at[6])
        part_copy(7, result.at[mine], result.at[mine], me ^ 1)

    contrib[...] = jnp.zeros_like(contrib)
    g2 = dot(gl_t[0:CLSP, :], two[...])
    for b in range(4):
        contrib[2 * HID + b * CLSP : 2 * HID + (b + 1) * CLSP, :] = g2[
            :, b * BLK : (b + 1) * BLK
        ].astype(BF16)

    def back_first(k, c):
        cut = at(k * CH, CH)
        grad = acc3[:, cut] + dot(ga_t[...], adj[:, cut])
        grad = grad + dot(w2_t[:, 0:HID], gl_t[:, cut])
        pre = dot_nt(w1_t[...], both[cut, :])
        sigma = 1.0 / (1.0 + jnp.exp(-pre))
        slope = sigma * (1.0 + pre * (1.0 - sigma))
        node = lax.broadcasted_iota(jnp.int32, (HID, CH), 1) + k * CH
        gp_t[:, cut] = jnp.where(node < size, grad * slope, 0.0).astype(BF16)
        return c

    for k in range(3):
        make_spread(k)
        send_spread(k)
    lax.fori_loop(0, NCH, back_first, 0)

    g1 = dot(gp_t[...], both[...])
    contrib[0:HID, :] = g1[:, 0:F_IN].astype(BF16)
    contrib[HID : 2 * HID, :] = g1[:, F_IN : 2 * F_IN].astype(BF16)
    reduce_pair()
    make_spread(3)
    reduce_plane()
    send_spread(3)
    reduce_z()
    wait_bytes(agg_in.at[pl.ds(0, HALO - SLOT)], rsem.at[1])

    def fresh(k, c):
        cut = at(k * CH, CH)
        pre = dot(halo[cut, :], w1[0:F_IN, :]) + dot(agg_in[cut, :], w1[F_IN : 2 * F_IN, :])
        stale[cut, :] = (pre / (1.0 + jnp.exp(-pre))).astype(BF16)
        return c

    lax.fori_loop(0, NCH, fresh, 0)
    give_fresh = pltpu.make_async_copy(stale, fh_hbm, local_sem.at[1])
    give_fresh.start()

    return_plane()
    own_spread = pltpu.make_async_copy(
        send3.at[piece_of(me)], fg_hbm.at[piece_of(me)], local_sem.at[0]
    )
    own_spread.start()

    return_pair()
    wait_bytes(result.at[other], rsem.at[7])

    gs1_ref[...] = jnp.transpose(result[0:HID, :].astype(F32))
    gn1_ref[...] = jnp.transpose(result[HID : 2 * HID, :].astype(F32))
    for b, (dst, half) in enumerate(((gs2_ref, 0), (gs2_ref, 1), (gn2_ref, 0), (gn2_ref, 1))):
        block = result[2 * HID + b * CLSP : 2 * HID + (b + 1) * CLSP, :].astype(F32)
        dst[:, half * BLK : (half + 1) * BLK] = block[0:CLS, :]
    gives = [
        pltpu.make_async_copy(src, dst, local_sem.at[2 + i])
        for i, (src, dst) in enumerate(
            ((gs1_ref, gs1_hbm), (gn1_ref, gn1_hbm), (gs2_ref, gs2_hbm), (gn2_ref, gn2_hbm))
        )
    ]
    for give in gives:
        give.start()

    wait_bytes(send1.at[pl.ds(0, HALO - SLOT)], ssem.at[0])
    wait_bytes(send2.at[pl.ds(0, HALO - SLOT)], ssem.at[1])
    wait_bytes(send3.at[pl.ds(0, HALO - SLOT)], ssem.at[2])
    wait_bytes(contrib.at[mine], ssem.at[3])
    wait_bytes(plane_in.at[pl.ds(0, 15 * PIECE)], ssem.at[4])
    wait_bytes(z_in.at[pl.ds(0, 3 * PIECE)], ssem.at[5])
    wait_bytes(result.at[pl.ds(0, 15 * PIECE)], ssem.at[6])
    wait_bytes(result.at[mine], ssem.at[7])
    own_spread.wait()
    give_fresh.wait()
    for give in gives:
        give.wait()
    wait_bytes(fg_hbm.at[pl.ds(0, HALO - SLOT)], rsem.at[2])


def hand_over(*refs):
    held, sems = refs[12:18], refs[18]
    into = [pltpu.make_async_copy(refs[i], held[i], sems.at[i]) for i in range(6)]
    out = [pltpu.make_async_copy(held[i], refs[6 + i], sems.at[6 + i]) for i in range(6)]
    for copy in into[::-1]:
        copy.start()
    for i in range(5, -1, -1):
        into[i].wait()
        out[i].start()
    for copy in out:
        copy.wait()


def local(
    features, self_one, neigh_one, self_two, neigh_two, tile_values, tile_rows, tile_cols,
    tile_count, part_size, send_rows, send_count, labels, train_mask, stale_hidden, stale_grads,
):
    def in_hbm(x):
        return pltpu.with_memory_space_constraint(x, pltpu.HBM)

    smem = pl.BlockSpec(memory_space=pltpu.SMEM)
    vmem = pl.BlockSpec(memory_space=pltpu.VMEM)
    hbm = pl.BlockSpec(memory_space=pltpu.HBM)
    packed = pl.pallas_call(
        prepare,
        out_shape=(
            jax.ShapeDtypeStruct((NODE, NODE + HALO), BF16),
            jax.ShapeDtypeStruct((HALO, HALF), BF16),
            jax.ShapeDtypeStruct((NODE, F_IN), BF16),
            jax.ShapeDtypeStruct((HALO, F_IN), BF16),
            jax.ShapeDtypeStruct((HALO, BLK), BF16),
            jax.ShapeDtypeStruct((PARTS, BLK), BF16),
        ),
        in_specs=[smem] * 4 + [hbm] * 4,
        out_specs=(vmem,) * 6,
        scratch_shapes=[
            pltpu.VMEM((TILES, BLK, BLK), BF16),
            pltpu.VMEM((TILES // 2, BLK, BLK), F32),
            pltpu.VMEM((HALF, 2 * F_IN), BF16),
            pltpu.VMEM((SLOT, PARTS), jnp.int32),
            pltpu.VMEM((PARTS, PARTS), jnp.int32),
            pltpu.SMEM((520,), jnp.int32),
            pltpu.SMEM((TILES // 2,), jnp.int32),
            pltpu.SemaphoreType.DMA((TILES // STAGE,)),
            pltpu.SemaphoreType.DMA((3,)),
        ],
        compiler_params=pltpu.CompilerParams(vmem_limit_bytes=20 * 1024 * 1024),
        cost_estimate=pl.CostEstimate(
            flops=1_500_000_000, bytes_accessed=8_000_000, transcendentals=0
        ),
        name="prepare",
    )(
        in_hbm(tile_rows), in_hbm(tile_cols), tile_count, part_size,
        *(in_hbm(x) for x in (tile_values, features, send_rows[0].T, send_count)),
    )
    outs = pl.pallas_call(
        step,
        out_shape=(
            pltpu.HBM((F_IN, HID), F32),
            pltpu.HBM((F_IN, HID), F32),
            pltpu.HBM((CLS, HID), F32),
            pltpu.HBM((CLS, HID), F32),
            pltpu.HBM((HALO, HID), BF16),
            pltpu.HBM((HALO, HID), BF16),
        ),
        in_specs=[smem] + [hbm] * 2 + [vmem] * 12,
        out_specs=(hbm,) * 6,
        scratch_shapes=[
            pltpu.VMEM((HALO, BLK), BF16),
            pltpu.VMEM((NODE, 2 * F_IN), BF16),
            pltpu.VMEM((HALF, 2 * F_IN), BF16),
            pltpu.VMEM((HALO, F_IN), BF16),
            pltpu.VMEM((NODE, 2 * HID), BF16),
            pltpu.VMEM((HALO, HID), BF16),
            pltpu.VMEM((HALO, HID), BF16),
            pltpu.VMEM((2, HID, HALO), BF16),
            pltpu.VMEM((NODE, F_IN), F32),
            pltpu.VMEM((NODE, HID), F32),
            pltpu.VMEM((HID, NODE), F32),
            pltpu.VMEM((HID, 2 * HID), BF16),
            pltpu.VMEM((HID, 2 * F_IN), BF16),
            pltpu.VMEM((HID, NODE), BF16),
            pltpu.VMEM((HID, NODE), BF16),
            pltpu.VMEM((HID, NODE), BF16),
            pltpu.VMEM((HALO, F_IN), BF16),
            pltpu.VMEM((HALO, F_IN), BF16),
            pltpu.VMEM((HALO, HID), BF16),
            pltpu.VMEM((2 * F_IN, HID), BF16),
            pltpu.VMEM((HID, 2 * HID), BF16),
            pltpu.VMEM((2 * SIDE, BLK), BF16),
            pltpu.VMEM((SIDE, BLK), BF16),
            pltpu.VMEM((SIDE, BLK), BF16),
            pltpu.VMEM((SIDE, BLK), BF16),
            pltpu.VMEM((4 * PIECE, BLK), BF16),
            pltpu.VMEM((2 * SIDE, BLK), BF16),
            pltpu.VMEM((F_IN, HID), F32),
            pltpu.VMEM((F_IN, HID), F32),
            pltpu.VMEM((CLS, HID), F32),
            pltpu.VMEM((CLS, HID), F32),
            pltpu.SemaphoreType.DMA((2,)),
            pltpu.SemaphoreType.DMA((8,)),
            pltpu.SemaphoreType.DMA((8,)),
            pltpu.SemaphoreType.DMA((6,)),
        ],
        compiler_params=pltpu.CompilerParams(
            collective_id=0, has_side_effects=True, vmem_limit_bytes=25 * 1024 * 1024
        ),
        cost_estimate=pl.CostEstimate(
            flops=20_000_000_000, bytes_accessed=8_000_000, transcendentals=2_000_000
        ),
        name="train_step",
    )(
        part_size, in_hbm(stale_hidden), in_hbm(stale_grads), *packed,
        self_one, neigh_one, self_two.T, neigh_two.T,
        labels.reshape(1, NODE), train_mask.reshape(1, NODE),
    )
    gs1, gn1, gs2, gn2, fresh_hidden, fresh_grads = pl.pallas_call(
        hand_over,
        out_shape=tuple(jax.ShapeDtypeStruct(o.shape, o.dtype) for o in outs),
        in_specs=[hbm] * 6,
        out_specs=(hbm,) * 6,
        scratch_shapes=[pltpu.VMEM(o.shape, o.dtype) for o in outs] + [pltpu.SemaphoreType.DMA((12,))],
        name="hand_over",
    )(*outs)
    return (gs1, gn1, gs2.T, gn2.T, fresh_hidden, fresh_grads)


def solution(mesh):
    part = P(("row", "col"))
    return jax.shard_map(
        local,
        mesh=mesh,
        in_specs=(
            part, P(), P(), P(), P(), part, part, part, part, part, part, P(), part, part, part, part,
        ),
        out_specs=(P(), P(), P(), P(), part, part),
        check_vma=False,
    )
```
